128 devices in a mesh: rows: 32 (over z_hi, x, y), feat: 4 (over z_lo, core).
Axes of the slice: x: 4, y: 4, z: 4 (z_hi: 2, z_lo: 2; z = z_hi * 2 + z_lo), core: 2. Of those that a mesh axis runs over, the one named last changes fastest.
Arguments:
- features: bfloat16 [256, 196608], P('feat', 'rows'), may hold values from -6 to 6
- weight: bfloat16 [256, 256], P('feat'), may hold values from -0.375 to 0.375
- cotangent: bfloat16 [256, 196608], P('feat', 'rows'), may hold values from -6 to 6
- blocks: bfloat16 [32, 256, 128, 128], P('rows', 'feat'), may hold values from -0.25 to 0.25
- row_block: int32 [32, 256], P('rows', 'feat'), may hold values from 0 to 47
- src_owner: int32 [32, 256, 1], P('rows', 'feat'), may hold values from 0 to 31; in each aligned block of 64 rows (0 to 63, 64 to 127, ..., all dimensions but the last counted through in order) at most 4 rows name the same one
- src_block: int32 [32, 256], P('rows', 'feat'), may hold values from 0 to 47
- live: int32 [32, 4], P('rows', 'feat'), may hold values from 8 to 64, as said below
Outputs:
- activation: bfloat16 [256, 196608], P('feat', 'rows')
- feature_grad: bfloat16 [256, 196608], P('feat', 'rows')
- weight_grad: float32 [256, 256], P('feat')
The draws below stay inside these ranges and needn't reach their ends.
Inputs may be any that keep to these rules, and one draw needn't show every extreme that they name: `src_owner`: among the 64 slots of one device, no owner is named more than 4 times, a bound that some block reaches. Some device has all 64 slots live.
All inputs are finite; a program needn't handle non-finite values.
Results may differ from the reference program's by a relative error of at most 0.024.
Values may be sent and summed in bfloat16 or wider, within the bound.
No kernel may reach another device: no remote copies, remote signals or barrier semaphores. Data moves between devices by JAX's collectives and lax.ppermute only.
A program may use at most 128 MiB of HBM per device.

```python
import math
import jax
import jax.numpy as jnp
import numpy as np
from jax import lax

HID = 256
BLK = 128
BR_DEV = 48
NB_DEV = 64
SLOTS = 256
CAP = 4
NODES = 196608
N_ROWS = 32
N_FEAT = 4


def draw_live(key, part):
    first_key, second_key = jax.random.split(jax.random.fold_in(key, 7))
    levels = jax.random.randint(first_key, (N_ROWS * N_FEAT,), 1, 9)
    chosen = jax.random.randint(second_key, (), 0, N_ROWS * N_FEAT)
    levels = jnp.where(jnp.arange(N_ROWS * N_FEAT) == chosen, 8, levels)
    return (levels * (NB_DEV // 8)).reshape(N_ROWS, N_FEAT).astype(jnp.int32)


def place_ends(result, rng, smallest, largest):
    extent = result.shape
    spot = [jax.random.randint(jax.random.fold_in(rng, axis), (), 0, extent[axis]) for axis in range(len(extent))]
    result = result.at[tuple(spot)].set(smallest)
    longest = extent.index(max(extent))
    spot[longest] = (spot[longest] + 1) % extent[longest]
    return result.at[tuple(spot)].set(largest)


def level_of(key, dims, cuts, low, largest):
    gain, own = 1.0, jax.random.fold_in(key, 6)
    for position, shards_of in cuts:
        draws = jnp.exp(jax.random.uniform(jax.random.fold_in(own, position), (shards_of,), jnp.float32, low / len(cuts), largest / len(cuts)))
        gain = gain * jnp.repeat(draws, dims[position] // shards_of).reshape([-1 if axis == position else 1 for axis in range(len(dims))])
    return gain


def shared_out(stream_key, own, number, rows, number_of, top, bound, lean):
    ranking = jax.random.permutation(stream_key, number_of)
    packed, usual = load_shares(number_of, rows * top, bound, lean, True), load_shares(number_of, rows * top, bound, lean, False)
    places = jnp.arange(number_of)

    def named(tallies, turn):
        used = int((tallies > 0).sum())
        fixed = max(1, used // 4)
        passed = fixed + (places - fixed + turn * (used - fixed)) % max(1, number_of - fixed)
        return jnp.zeros((number_of,), jnp.int32).at[ranking[jnp.where(places < fixed, places, passed)]].set(jnp.asarray(tallies, jnp.int32))

    tallies = jnp.where(number % 4 == 0, named(packed, number // 4), named(usual, number - number // 4 - 1))
    mixed = jax.random.permutation(jax.random.fold_in(own, 3), number_of)
    donor, receiver = mixed[0:number_of // 2 * 2:2], mixed[1:number_of // 2 * 2:2]
    room = jnp.minimum(tallies[donor] - 1, bound - tallies[receiver]) // 2
    room = jnp.where((donor == ranking[0]) | (receiver == ranking[0]) | (tallies[receiver] == 0), 0, jnp.maximum(room, 0))
    passed = jax.random.randint(jax.random.fold_in(own, 4), (number_of // 2,), 0, 1 << 20) % (room + 1)
    tallies = tallies.at[donor].add(-passed).at[receiver].add(passed)
    items = jnp.searchsorted(jnp.cumsum(tallies), jnp.arange(rows * top), side="right").astype(jnp.int32)
    grid = items.reshape(top, rows).T
    grid = grid[jax.random.permutation(jax.random.fold_in(own, 1), rows)]
    turn = jax.random.randint(jax.random.fold_in(own, 2), (rows, 1), 0, top)
    return jnp.take_along_axis(grid, (jnp.arange(top)[None, :] + turn) % top, axis=1)


def load_shares(amount, total, most, lean, full):
    weights = [(1 << 20) // math.isqrt(standing ** lean) + 1 for standing in range(1, amount + 1)]
    largest = most if full else min(most, max(-(-total // amount), total * weights[0] // sum(weights)))
    least = 1 if total - largest >= amount - 1 else 0
    given, spare = [largest] + [least] * (amount - 1), total - largest - least * (amount - 1)
    while spare > 0:
        candidates = [i for i in range(1, amount) if given[i] < largest] or [i for i in range(1, amount) if given[i] < most]
        pool, remaining = sum([weights[i] for i in candidates]), spare
        for i in candidates:
            extra = min(most - given[i], max(1, remaining * weights[i] // pool), spare)
            given[i] = given[i] + extra
            spare = spare - extra
    return np.array(given)


def noise(rng, extent, scale, most, cuts=(), held_as=jnp.bfloat16):
    array = jax.random.normal(rng, extent, jnp.float32) * scale
    if len(cuts) > 0:
        array = level_of(rng, extent, cuts, -0.22, 0.18) * array
    return jnp.clip(array, min=-most, max=most).astype(held_as)


def setup_inputs(seed: int = 0) -> dict:
    key_list = jax.random.split(jax.random.key(seed), 9)
    features = noise(key_list[0], (HID, NODES), 1.0, 6.0, ((0, 4), (1, 32)))
    weight = noise(key_list[1], (HID, HID), HID ** -0.5, 0.375, ((0, 4),))
    cotangent = noise(key_list[2], (HID, NODES), 1.0, 6.0, ((0, 4), (1, 32)))
    blocks = noise(key_list[3], (N_ROWS, SLOTS, BLK, BLK), (4 * BLK) ** -0.5, 0.25, ((0, 32), (1, 4)))
    row_block = place_ends(jax.random.randint(key_list[4], (N_ROWS, SLOTS), 0, BR_DEV), jax.random.fold_in(key_list[4], 1), 0, BR_DEV - 1).astype(jnp.int32)
    src_owner_keys = jax.random.split(jax.random.fold_in(key_list[5], 1), N_ROWS * SLOTS // NB_DEV)
    src_owner_turns = jax.random.permutation(jax.random.fold_in(key_list[5], 3), N_ROWS * SLOTS // NB_DEV)
    src_owner = jax.vmap(lambda own, number: shared_out(jax.random.fold_in(key_list[5], 2), own, number, NB_DEV, N_ROWS, 1, CAP, 2))(src_owner_keys, src_owner_turns).reshape((N_ROWS, SLOTS, 1))
    src_block = place_ends(jax.random.randint(key_list[6], (N_ROWS, SLOTS), 0, BR_DEV), jax.random.fold_in(key_list[6], 1), 0, BR_DEV - 1).astype(jnp.int32)
    live = draw_live(jax.random.fold_in(key_list[8], 71), 0)
    return dict(features=features, weight=weight, cotangent=cotangent, blocks=blocks, row_block=row_block, src_owner=src_owner, src_block=src_block, live=live)


def owner_slots(blocks, row_block, src_owner, src_block, live, owner):
    slot_ids = jnp.arange(SLOTS, dtype=jnp.int32)
    counts = live[owner]
    living = slot_ids % NB_DEV < counts[slot_ids // NB_DEV]
    masked_tiles = blocks[owner] * living.astype(jnp.bfloat16)[:, None, None]
    columns = src_owner[owner, :, 0] * BR_DEV + src_block[owner]
    return (masked_tiles, columns.astype(jnp.int32), row_block[owner].astype(jnp.int32))

def reference(features, weight, cotangent, blocks, row_block, src_owner, src_block, live):
    block_total = N_ROWS * BR_DEV
    feature_blocks = features.reshape(HID, block_total, BLK)

    def forward_owner(owner):
        masked_tiles, columns, targets = owner_slots(blocks, row_block, src_owner, src_block, live, owner)
        picked = feature_blocks[:, columns, :].astype(jnp.float32)
        products = jnp.einsum('fsm,snm->fsn', picked, masked_tiles.astype(jnp.float32))
        return jnp.zeros((HID, BR_DEV, BLK), jnp.float32).at[:, targets, :].add(products)
    stacked = lax.map(forward_owner, jnp.arange(N_ROWS, dtype=jnp.int32))
    aggregated = jnp.transpose(stacked, (1, 0, 2, 3)).reshape(HID, NODES).astype(jnp.bfloat16)
    preact = jnp.dot(weight, aggregated, preferred_element_type=jnp.float32)
    positive = jnp.maximum(preact, 0.0)
    activation = (positive * positive).astype(jnp.bfloat16)
    pre_grad = (2.0 * cotangent.astype(jnp.float32) * positive).astype(jnp.bfloat16)
    weight_grad = lax.dot_general(pre_grad, aggregated, (((1,), (1,)), ((), ())), preferred_element_type=jnp.float32) * (1.0 / math.sqrt(NODES))
    agg_grad = lax.dot_general(weight, pre_grad, (((0,), (0,)), ((), ())), preferred_element_type=jnp.float32).astype(jnp.bfloat16)
    grad_blocks = agg_grad.reshape(HID, N_ROWS, BR_DEV, BLK)

    def backward_owner(collected, owner):
        masked_tiles, columns, targets = owner_slots(blocks, row_block, src_owner, src_block, live, owner)
        owned = lax.dynamic_index_in_dim(grad_blocks, owner, 1, keepdims=False)
        gathered_rows = owned[:, targets, :].astype(jnp.float32)
        returned = jnp.einsum('fsn,snm->fsm', gathered_rows, masked_tiles.astype(jnp.float32)).astype(jnp.bfloat16)
        return (collected.at[:, columns, :].add(returned.astype(jnp.float32)), None)
    collected, _ = lax.scan(backward_owner, jnp.zeros((HID, block_total, BLK), jnp.float32), jnp.arange(N_ROWS, dtype=jnp.int32))
    feature_grad = collected.reshape(HID, NODES).astype(jnp.bfloat16)
    return (activation, feature_grad, weight_grad)
```

```python
import functools
import math

import jax
import jax.numpy as jnp
from jax import lax
from jax.experimental import pallas as pl
from jax.experimental.pallas import tpu as pltpu
from jax.sharding import PartitionSpec as P

BF = jnp.bfloat16
F32 = jnp.float32
I32 = jnp.int32
VMEM_LIMIT = 56 * 1024 * 1024
GROUP = 8


def params():
    return pltpu.CompilerParams(vmem_limit_bytes=VMEM_LIMIT)


def core_swap(x):
    return lax.ppermute(x, "feat", [(0, 1), (1, 0), (2, 3), (3, 2)])


def chip_swap(x):
    return lax.ppermute(x, "feat", [(0, 2), (2, 0), (1, 3), (3, 1)])


def gather_feat(x):
    far = chip_swap(x)
    return (x, core_swap(x), far, core_swap(far))


def relative(x, axis, me):
    a = jnp.split(x, 4, axis=axis)
    low = (me & 1) == 1
    high = (me & 2) == 2
    b = [jnp.where(low, a[i ^ 1], a[i]) for i in range(4)]
    c = [jnp.where(high, b[i ^ 2], b[i]) for i in range(4)]
    return jnp.concatenate(c, axis=axis)


def exact_dot(a, b):
    return jnp.dot(a.astype(BF), b.astype(BF), preferred_element_type=F32)


def ranks(want):
    n = want.shape[-1]
    upper = jnp.arange(n)[:, None] < jnp.arange(n)[None, :]
    return exact_dot(want, upper).astype(I32)


def serve_kernel(capacity, index, features, out):
    row = pl.program_id(0)
    width = features.shape[0]
    for k in range(capacity):
        start = pl.multiple_of(index[row * capacity + k] * 128, 128)
        out[0, k * width : (k + 1) * width, :] = features[:, pl.ds(start, 128)]


def serve(features, index, rows, capacity):
    width, nodes = features.shape
    return pl.pallas_call(
        functools.partial(serve_kernel, capacity),
        grid_spec=pltpu.PrefetchScalarGridSpec(
            num_scalar_prefetch=1,
            grid=(rows,),
            in_specs=[pl.BlockSpec((width, nodes), lambda r, i: (0, 0))],
            out_specs=pl.BlockSpec((1, capacity * width, 128), lambda r, i: (r, 0, 0)),
        ),
        out_shape=jax.ShapeDtypeStruct((rows, capacity * width, 128), BF),
        compiler_params=params(),
        cost_estimate=pl.CostEstimate(
            flops=0, bytes_accessed=rows * capacity * width * 256, transcendentals=0
        ),
    )(index, features)


def aggregate_kernel(lists, slots, source, target, live, panels, *refs):
    tiles = refs[:lists]
    out, held, panel, acc, sems = refs[lists:]
    blocks = out.shape[0]
    copies = [pltpu.make_async_copy(panels, panel, sems.at[lists])]
    copies += [pltpu.make_async_copy(tiles[j], held.at[j], sems.at[j]) for j in range(lists)]
    for c in copies:
        c.start()
    acc[...] = jnp.zeros_like(acc)
    copies[0].wait()
    for j in range(lists):
        copies[j + 1].wait()

        def body(g, carry, j=j):
            base = g * GROUP
            products = []
            for u in range(GROUP):
                s = j * slots + base + u
                products.append(
                    lax.dot_general(
                        panel[source[s]],
                        held[j, base + u],
                        (((1,), (1,)), ((), ())),
                        preferred_element_type=F32,
                    )
                )
            for u in range(GROUP):
                t = target[j * slots + base + u]
                acc[t] = acc[t] + products[u]
            return carry

        lax.fori_loop(0, (live[j] + GROUP - 1) // GROUP, body, 0)
    out[...] = acc[:blocks].astype(BF)


def aggregate(panels, tiles, source, target, live, blocks):
    lists = len(tiles)
    slots, size, _ = tiles[0].shape
    entries, width, _ = panels.shape
    any_spec = pl.BlockSpec(memory_space=pl.ANY)
    return pl.pallas_call(
        functools.partial(aggregate_kernel, lists, slots),
        grid_spec=pltpu.PrefetchScalarGridSpec(
            num_scalar_prefetch=3,
            grid=(1,),
            in_specs=[any_spec] * (lists + 1),
            out_specs=pl.BlockSpec((blocks, width, size), lambda i, *_: (0, 0, 0)),
            scratch_shapes=[
                pltpu.VMEM((lists, slots, size, size), BF),
                pltpu.VMEM((entries, width, size), BF),
                pltpu.VMEM((blocks + 1, width, size), F32),
                pltpu.SemaphoreType.DMA((lists + 1,)),
            ],
        ),
        out_shape=jax.ShapeDtypeStruct((blocks, width, size), BF),
        compiler_params=params(),
        cost_estimate=pl.CostEstimate(
            flops=2 * lists * slots * width * size * size,
            bytes_accessed=entries * width * size * 2 + lists * slots * size * size * 2,
            transcendentals=0,
        ),
    )(source, target, live, panels, *tiles)


def middle_kernel(step, weight, a0, a1, a2, a3, c0, c1, c2, c3, act, grad, wgrad):
    width = a0.shape[1]
    x = jnp.concatenate(
        [jnp.concatenate([a[b] for b in range(step)], axis=1) for a in (a0, a1, a2, a3)], axis=0
    )
    w = weight[...]
    preact = jnp.dot(w, x, preferred_element_type=F32)
    positive = jnp.maximum(preact, 0.0)
    own = positive[:width]
    act[...] = (own * own).astype(BF)
    cot = jnp.concatenate([c[...] for c in (c0, c1, c2, c3)], axis=0)
    pre = (2.0 * cot.astype(F32) * positive).astype(BF)
    g = lax.dot_general(
        w[:, :width], pre, (((0,), (0,)), ((), ())), preferred_element_type=F32
    ).astype(BF)
    for b in range(step):
        grad[b] = g[:, b * 128 : (b + 1) * 128]
    part = lax.dot_general(
        pre[:width], x, (((1,), (1,)), ((), ())), preferred_element_type=F32
    )

    @pl.when(pl.program_id(0) == 0)
    def _():
        wgrad[...] = part

    @pl.when(pl.program_id(0) > 0)
    def _():
        wgrad[...] = wgrad[...] + part


def middle(weight, aggregated, cotangent):
    blocks, width, size = aggregated[0].shape
    hidden = weight.shape[0]
    step = 8 if blocks % 8 == 0 else 1
    a_spec = pl.BlockSpec((step, width, size), lambda i: (i, 0, 0))
    c_spec = pl.BlockSpec((width, step * size), lambda i: (0, i))
    w_spec = pl.BlockSpec((width, hidden), lambda i: (0, 0))
    return pl.pallas_call(
        functools.partial(middle_kernel, step),
        grid=(blocks // step,),
        in_specs=[pl.BlockSpec((hidden, hidden), lambda i: (0, 0))] + [a_spec] * 4 + [c_spec] * 4,
        out_specs=[c_spec, a_spec, w_spec],
        out_shape=[
            jax.ShapeDtypeStruct((width, blocks * size), BF),
            jax.ShapeDtypeStruct((blocks, width, size), BF),
            jax.ShapeDtypeStruct((width, hidden), F32),
        ],
        compiler_params=params(),
        cost_estimate=pl.CostEstimate(
            flops=2 * hidden * (hidden + 2 * width) * blocks * size,
            bytes_accessed=10 * blocks * width * size * 2,
            transcendentals=0,
        ),
    )(weight, *aggregated, *cotangent)


def terms_kernel(lists, slots, dest, target, again, live, grads, *refs):
    tiles = refs[:lists]
    out, held, made, sems = refs[lists:]
    entries = out.shape[0]
    copies = [pltpu.make_async_copy(tiles[j], held.at[j], sems.at[j]) for j in range(lists)]
    for c in copies:
        c.start()
    for j in range(lists):
        copies[j].wait()

        def body(g, carry, j=j):
            base = g * GROUP
            products = []
            for u in range(GROUP):
                s = j * slots + base + u
                products.append(
                    jnp.dot(grads[target[s]], held[j, base + u], preferred_element_type=F32)
                )
            for u in range(GROUP):
                s = j * slots + base + u
                d = dest[s]
                kept = jnp.where(again[s] > 0, made[d].astype(F32), 0.0)
                made[d] = (kept + products[u]).astype(BF)
            return carry

        lax.fori_loop(0, (live[j] + GROUP - 1) // GROUP, body, 0)
    last = pltpu.make_async_copy(made.at[pl.ds(0, entries)], out, sems.at[lists])
    last.start()
    last.wait()


def terms(grads, tiles, dest, target, again, live, entries):
    lists = len(tiles)
    slots, size, _ = tiles[0].shape
    blocks, width, _ = grads.shape
    any_spec = pl.BlockSpec(memory_space=pl.ANY)
    return pl.pallas_call(
        functools.partial(terms_kernel, lists, slots),
        grid_spec=pltpu.PrefetchScalarGridSpec(
            num_scalar_prefetch=4,
            grid=(1,),
            in_specs=[pl.BlockSpec((blocks, width, size), lambda i, *_: (0, 0, 0))]
            + [any_spec] * lists,
            out_specs=any_spec,
            scratch_shapes=[
                pltpu.VMEM((lists, slots, size, size), BF),
                pltpu.VMEM((entries + 1, width, size), BF),
                pltpu.SemaphoreType.DMA((lists + 1,)),
            ],
        ),
        out_shape=jax.ShapeDtypeStruct((entries, width, size), BF),
        compiler_params=params(),
        cost_estimate=pl.CostEstimate(
            flops=2 * lists * slots * width * size * size,
            bytes_accessed=entries * width * size * 2 + lists * slots * size * size * 2,
            transcendentals=0,
        ),
    )(dest, target, again, live, grads, *tiles)


def collect_kernel(capacity, blocks, index, count, incoming, out, acc):
    row = pl.program_id(0)
    width = out.shape[0]

    @pl.when(row == 0)
    def _():
        acc[...] = jnp.zeros_like(acc)

    def body(g, carry):
        for u in range(4):
            k = g * 4 + u
            t = index[row * capacity + k]
            start = pl.multiple_of(k * width, width)
            acc[t] = acc[t] + incoming[0, pl.ds(start, width), :].astype(F32)
        return carry

    lax.fori_loop(0, (count[row] + 3) // 4, body, 0)

    @pl.when(row == pl.num_programs(0) - 1)
    def _():
        for b in range(blocks):
            out[:, b * 128 : (b + 1) * 128] = acc[b].astype(BF)


def collect(incoming, index, count, blocks, width, capacity):
    rows = incoming.shape[0]
    return pl.pallas_call(
        functools.partial(collect_kernel, capacity, blocks),
        grid_spec=pltpu.PrefetchScalarGridSpec(
            num_scalar_prefetch=2,
            grid=(rows,),
            in_specs=[pl.BlockSpec((1, capacity * width, 128), lambda r, *_: (r, 0, 0))],
            out_specs=pl.BlockSpec((width, blocks * 128), lambda r, *_: (0, 0)),
            scratch_shapes=[pltpu.VMEM((blocks + 1, width, 128), F32)],
        ),
        out_shape=jax.ShapeDtypeStruct((width, blocks * 128), BF),
        compiler_params=params(),
        cost_estimate=pl.CostEstimate(
            flops=rows * capacity * width * 128,
            bytes_accessed=rows * capacity * width * 256,
            transcendentals=0,
        ),
    )(index, count, incoming)


def exchange(x):
    return lax.all_to_all(x, "rows", split_axis=0, concat_axis=0, tiled=True)


def on_device(features, weight, cotangent, blocks, row_block, src_owner, src_block, live):
    rows = lax.axis_size("rows")
    feats = lax.axis_size("feat")
    me = lax.axis_index("feat")
    width, nodes = features.shape
    size = blocks.shape[2]
    slots = blocks.shape[1]
    local = nodes // size
    capacity = max(2, 2 * slots // rows) * feats

    tiles = gather_feat(blocks[0])

    here = jnp.arange(slots, dtype=I32)
    alive = here < live[0, 0]
    code = jnp.where(alive, src_owner[0, :, 0] * 64 + src_block[0], -1)
    goal = jnp.where(alive, row_block[0], local)
    note = gather_feat(jnp.stack([code, goal]))
    code = jnp.concatenate([n[0] for n in note])
    target = jnp.concatenate([n[1] for n in note])
    valid = code >= 0
    counts = jnp.stack([jnp.sum((n[0] >= 0).astype(I32)) for n in note])
    owner = jnp.where(valid, code >> 6, -1)
    block = jnp.where(valid, code & 63, -1)
    owner_hot = owner[:, None] == jnp.arange(rows, dtype=I32)[None, :]
    block_hot = block[:, None] == jnp.arange(local, dtype=I32)[None, :]
    want = exact_dot(owner_hot.T, block_hot) > 0.5
    rank = ranks(want)
    request = jnp.pad(want.astype(I32), ((0, 0), (0, 128 - local)))
    asked = exchange(request)[:, :local]
    asked_rank = ranks(asked)
    asked_count = jnp.sum(asked, axis=1)
    at = jnp.arange(capacity, dtype=I32)[None, :, None]
    chosen = (asked[:, None, :] > 0) & (asked_rank[:, None, :] == at)
    index = jnp.sum(jnp.where(chosen, jnp.arange(local, dtype=I32), 0), axis=2)
    index_flat = index.reshape(-1)
    index_sum = jnp.where(
        jnp.arange(capacity, dtype=I32)[None, :] < asked_count[:, None], index, local
    ).reshape(-1)

    slot_rank = jnp.sum(jnp.where(block_hot, exact_dot(owner_hot, rank), 0.0), axis=1).astype(I32)
    place = owner * capacity + slot_rank
    source = jnp.where(valid, place, 0)
    dest = jnp.where(valid, place, rows * capacity)
    order = jnp.arange(feats * slots, dtype=I32)
    again = jnp.any(
        (code[:, None] == code[None, :]) & (order[None, :] < order[:, None]), axis=1
    ).astype(I32)

    weights = relative(jnp.concatenate(gather_feat(weight), axis=0), 1, me)
    cotangents = gather_feat(cotangent)

    served = serve(features, index_flat, rows, capacity)
    panels = exchange(served).reshape(rows * capacity, width, size)
    own = aggregate(panels, tiles, source, target, counts, local)
    aggregated = gather_feat(own)
    activation, grads, weight_part = middle(weights, aggregated, cotangents)
    made = terms(grads, tiles, dest, target, again, counts, rows * capacity)
    returned = exchange(made.reshape(rows, capacity * width, size))

    total = relative(weight_part, 1, me)
    step = 1
    while step < rows:
        total = total + lax.ppermute(total, "rows", [(i, i ^ step) for i in range(rows)])
        step *= 2
    weight_grad = total * (1.0 / math.sqrt(nodes * rows))
    feature_grad = collect(returned, index_sum, asked_count, local, width, capacity)
    return (activation, feature_grad, weight_grad)


def solution(mesh):
    placed = (
        P("feat", "rows"),
        P("feat", None),
        P("feat", "rows"),
        P("rows", "feat", None, None),
        P("rows", "feat"),
        P("rows", "feat", None),
        P("rows", "feat"),
        P("rows", "feat"),
    )
    return jax.shard_map(
        on_device,
        mesh=mesh,
        in_specs=placed,
        out_specs=(P("feat", "rows"), P("feat", "rows"), P("feat", None)),
        check_vma=False,
    )
```

```python
import functools
import math

import jax
import jax.numpy as jnp
from jax import lax
from jax.experimental import pallas as pl
from jax.experimental.pallas import tpu as pltpu
from jax.sharding import PartitionSpec as P

BF = jnp.bfloat16
F32 = jnp.float32
I32 = jnp.int32
VMEM_LIMIT = 56 * 1024 * 1024
GROUP = 8
STRIDE = 16
CAPACITIES = (8, 11, 12, 13, 14)


def params():
    return pltpu.CompilerParams(vmem_limit_bytes=VMEM_LIMIT)


def core_swap(x):
    return lax.ppermute(x, "feat", [(0, 1), (1, 0), (2, 3), (3, 2)])


def chip_swap(x):
    return lax.ppermute(x, "feat", [(0, 2), (2, 0), (1, 3), (3, 1)])


def gather_feat(x):
    far = chip_swap(x)
    return (x, core_swap(x), far, core_swap(far))


def relative(x, axis, me):
    a = jnp.split(x, 4, axis=axis)
    low = (me & 1) == 1
    high = (me & 2) == 2
    b = [jnp.where(low, a[i ^ 1], a[i]) for i in range(4)]
    c = [jnp.where(high, b[i ^ 2], b[i]) for i in range(4)]
    return jnp.concatenate(c, axis=axis)


def exact_dot(a, b):
    return jnp.dot(a.astype(BF), b.astype(BF), preferred_element_type=F32)


def ranks(want):
    n = want.shape[-1]
    upper = jnp.arange(n)[:, None] < jnp.arange(n)[None, :]
    return exact_dot(want, upper).astype(I32)


def serve_kernel(step, index, count, features, out):
    width = features.shape[0]
    for i in range(step):
        row = pl.program_id(0) * step + i

        def body(k, carry, i=i, row=row):
            start = pl.multiple_of(index[row * STRIDE + k] * 128, 128)
            to = pl.multiple_of(k * width, width)
            out[i, pl.ds(to, width), :] = features[:, pl.ds(start, 128)]
            return carry

        lax.fori_loop(0, count[row], body, 0)


def serve(features, index, count, rows, capacity):
    width, nodes = features.shape
    step = 4
    return pl.pallas_call(
        functools.partial(serve_kernel, step),
        grid_spec=pltpu.PrefetchScalarGridSpec(
            num_scalar_prefetch=2,
            grid=(rows // step,),
            in_specs=[pl.BlockSpec((width, nodes), lambda r, *_: (0, 0))],
            out_specs=pl.BlockSpec((step, capacity * width, 128), lambda r, *_: (r, 0, 0)),
        ),
        out_shape=jax.ShapeDtypeStruct((rows, capacity * width, 128), BF),
        compiler_params=params(),
        cost_estimate=pl.CostEstimate(
            flops=0, bytes_accessed=rows * capacity * width * 256, transcendentals=0
        ),
    )(index, count, features)


def tile_copies(lists, tiles, held, sems):
    copies, n = [], 0
    for j in range(lists[0]):
        group = []
        for piece, start, size in lists[1][j]:
            group.append(
                pltpu.make_async_copy(
                    tiles[piece], held.at[j, pl.ds(start, size)], sems.at[n]
                )
            )
            n += 1
        copies.append(group)
    return copies


def entry(place, capacity):
    return (place >> 6) * capacity + (place & 63)


def aggregate_kernel(lists, slots, capacity, place, target, live, panels, *refs):
    pieces = sum(len(x) for x in lists[1])
    tiles = refs[:pieces]
    out, held, panel, acc, sems = refs[pieces:]
    blocks = out.shape[0]
    entries = panels.shape[0]
    first = pltpu.make_async_copy(panels, panel.at[pl.ds(0, entries)], sems.at[pieces])
    first.start()
    copies = tile_copies(lists, tiles, held, sems)
    for group in copies:
        for c in group:
            c.start()
    acc[...] = jnp.zeros_like(acc)
    first.wait()
    for j in range(lists[0]):
        for c in copies[j]:
            c.wait()

        def body(g, carry, j=j):
            base = g * GROUP
            products = []
            for u in range(GROUP):
                s = j * slots + base + u
                products.append(
                    lax.dot_general(
                        panel[entry(place[s], capacity)],
                        held[j, base + u],
                        (((1,), (1,)), ((), ())),
                        preferred_element_type=F32,
                    )
                )
            for u in range(GROUP):
                t = target[j * slots + base + u]
                acc[t] = acc[t] + products[u]
            return carry

        lax.fori_loop(0, (live[j] + GROUP - 1) // GROUP, body, 0)
    out[...] = acc[:blocks].astype(BF)


def aggregate(panels, tiles, lists, slots, place, target, live, blocks, capacity):
    size = tiles[0].shape[1]
    entries, width, _ = panels.shape
    any_spec = pl.BlockSpec(memory_space=pl.ANY)
    return pl.pallas_call(
        functools.partial(aggregate_kernel, lists, slots, capacity),
        grid_spec=pltpu.PrefetchScalarGridSpec(
            num_scalar_prefetch=3,
            grid=(1,),
            in_specs=[any_spec] * (len(tiles) + 1),
            out_specs=pl.BlockSpec((blocks, width, size), lambda i, *_: (0, 0, 0)),
            scratch_shapes=[
                pltpu.VMEM((lists[0], slots, size, size), BF),
                pltpu.VMEM((entries + 1, width, size), BF),
                pltpu.VMEM((blocks + 1, width, size), F32),
                pltpu.SemaphoreType.DMA((len(tiles) + 1,)),
            ],
        ),
        out_shape=jax.ShapeDtypeStruct((blocks, width, size), BF),
        compiler_params=params(),
        cost_estimate=pl.CostEstimate(
            flops=2 * lists[0] * slots * width * size * size,
            bytes_accessed=entries * width * size * 2 + lists[0] * slots * size * size * 2,
            transcendentals=0,
        ),
    )(place, target, live, panels, *tiles)


def middle_kernel(step, weight, a0, a1, a2, a3, c0, c1, c2, c3, act, grad, wgrad):
    width = a0.shape[1]
    x = jnp.concatenate(
        [jnp.concatenate([a[b] for b in range(step)], axis=1) for a in (a0, a1, a2, a3)], axis=0
    )
    w = weight[...]
    preact = jnp.dot(w, x, preferred_element_type=F32)
    positive = jnp.maximum(preact, 0.0)
    own = positive[:width]
    act[...] = (own * own).astype(BF)
    cot = jnp.concatenate([c[...] for c in (c0, c1, c2, c3)], axis=0)
    pre = (2.0 * cot.astype(F32) * positive).astype(BF)
    g = lax.dot_general(
        w[:, :width], pre, (((0,), (0,)), ((), ())), preferred_element_type=F32
    ).astype(BF)
    for b in range(step):
        grad[b] = g[:, b * 128 : (b + 1) * 128]
    part = lax.dot_general(
        pre[:width], x, (((1,), (1,)), ((), ())), preferred_element_type=F32
    )

    @pl.when(pl.program_id(0) == 0)
    def _():
        wgrad[...] = part

    @pl.when(pl.program_id(0) > 0)
    def _():
        wgrad[...] = wgrad[...] + part


def middle(weight, aggregated, cotangent):
    blocks, width, size = aggregated[0].shape
    hidden = weight.shape[0]
    step = 8 if blocks % 8 == 0 else 1
    a_spec = pl.BlockSpec((step, width, size), lambda i: (i, 0, 0))
    c_spec = pl.BlockSpec((width, step * size), lambda i: (0, i))
    w_spec = pl.BlockSpec((width, hidden), lambda i: (0, 0))
    return pl.pallas_call(
        functools.partial(middle_kernel, step),
        grid=(blocks // step,),
        in_specs=[pl.BlockSpec((hidden, hidden), lambda i: (0, 0))] + [a_spec] * 4 + [c_spec] * 4,
        out_specs=[c_spec, a_spec, w_spec],
        out_shape=[
            jax.ShapeDtypeStruct((width, blocks * size), BF),
            jax.ShapeDtypeStruct((blocks, width, size), BF),
            jax.ShapeDtypeStruct((width, hidden), F32),
        ],
        compiler_params=params(),
        cost_estimate=pl.CostEstimate(
            flops=2 * hidden * (hidden + 2 * width) * blocks * size,
            bytes_accessed=10 * blocks * width * size * 2,
            transcendentals=0,
        ),
    )(weight, *aggregated, *cotangent)


def terms_kernel(lists, slots, capacity, place, target, again, live, grads, *refs):
    pieces = sum(len(x) for x in lists[1])
    tiles = refs[:pieces]
    out, held, made, sems = refs[pieces:]
    entries = out.shape[0]
    copies = tile_copies(lists, tiles, held, sems)
    for group in copies:
        for c in group:
            c.start()
    for j in range(lists[0]):
        for c in copies[j]:
            c.wait()

        def body(g, carry, j=j):
            base = g * GROUP
            products = []
            for u in range(GROUP):
                s = j * slots + base + u
                t = jnp.minimum(target[s], grads.shape[0] - 1)
                products.append(
                    jnp.dot(grads[t], held[j, base + u], preferred_element_type=F32)
                )
            for u in range(GROUP):
                s = j * slots + base + u
                d = entry(place[s], capacity)
                kept = jnp.where(again[s] > 0, made[d].astype(F32), 0.0)
                made[d] = (kept + products[u]).astype(BF)
            return carry

        lax.fori_loop(0, (live[j] + GROUP - 1) // GROUP, body, 0)
    last = pltpu.make_async_copy(made.at[pl.ds(0, entries)], out, sems.at[pieces])
    last.start()
    last.wait()


def terms(grads, tiles, lists, slots, place, target, again, live, rows, capacity):
    entries = rows * capacity
    size = tiles[0].shape[1]
    blocks, width, _ = grads.shape
    any_spec = pl.BlockSpec(memory_space=pl.ANY)
    return pl.pallas_call(
        functools.partial(terms_kernel, lists, slots, capacity),
        grid_spec=pltpu.PrefetchScalarGridSpec(
            num_scalar_prefetch=4,
            grid=(1,),
            in_specs=[pl.BlockSpec((blocks, width, size), lambda i, *_: (0, 0, 0))]
            + [any_spec] * len(tiles),
            out_specs=any_spec,
            scratch_shapes=[
                pltpu.VMEM((lists[0], slots, size, size), BF),
                pltpu.VMEM((entries + 1, width, size), BF),
                pltpu.SemaphoreType.DMA((len(tiles) + 1,)),
            ],
        ),
        out_shape=jax.ShapeDtypeStruct((entries, width, size), BF),
        compiler_params=params(),
        cost_estimate=pl.CostEstimate(
            flops=2 * lists[0] * slots * width * size * size,
            bytes_accessed=entries * width * size * 2 + lists[0] * slots * size * size * 2,
            transcendentals=0,
        ),
    )(place, target, again, live, grads, *tiles)


def collect_kernel(step, blocks, index, count, incoming, out, acc):
    width = out.shape[0]

    @pl.when(pl.program_id(0) == 0)
    def _():
        acc[...] = jnp.zeros_like(acc)

    for i in range(step):
        row = pl.program_id(0) * step + i

        def body(k, carry, i=i, row=row):
            t = index[row * STRIDE + k]
            start = pl.multiple_of(k * width, width)
            acc[t] = acc[t] + incoming[i, pl.ds(start, width), :].astype(F32)
            return carry

        lax.fori_loop(0, count[row], body, 0)

    @pl.when(pl.program_id(0) == pl.num_programs(0) - 1)
    def _():
        for b in range(blocks):
            out[:, b * 128 : (b + 1) * 128] = acc[b].astype(BF)


def collect(incoming, index, count, blocks, width, capacity):
    rows = incoming.shape[0]
    step = 4
    return pl.pallas_call(
        functools.partial(collect_kernel, step, blocks),
        grid_spec=pltpu.PrefetchScalarGridSpec(
            num_scalar_prefetch=2,
            grid=(rows // step,),
            in_specs=[pl.BlockSpec((step, capacity * width, 128), lambda r, *_: (r, 0, 0))],
            out_specs=pl.BlockSpec((width, blocks * 128), lambda r, *_: (0, 0)),
            scratch_shapes=[pltpu.VMEM((blocks, width, 128), F32)],
        ),
        out_shape=jax.ShapeDtypeStruct((width, blocks * 128), BF),
        compiler_params=params(),
        cost_estimate=pl.CostEstimate(
            flops=rows * capacity * width * 128,
            bytes_accessed=rows * capacity * width * 256,
            transcendentals=0,
        ),
    )(index, count, incoming)


def exchange(x):
    return lax.all_to_all(x, "rows", split_axis=0, concat_axis=0, tiled=True)


def tree_sum(parts):
    while len(parts) > 1:
        parts = [parts[i] + parts[i + 1] for i in range(0, len(parts), 2)]
    return parts[0]


def sum_rows(x, rows):
    low = 4
    for steps in (range(low), range(0, rows, low)):
        x = x.astype(BF)
        parts = [
            lax.ppermute(x, "rows", [(i, i ^ step) for i in range(rows)]) if step else x
            for step in steps
        ]
        x = tree_sum([p.astype(F32) for p in parts])
    return x


def body(
    capacity,
    rows,
    feats,
    features,
    own_tiles,
    far_head,
    weights,
    cotangent,
    code,
    target,
    rank,
    asked,
):
    width, nodes = features.shape
    slots, size, _ = own_tiles.shape
    local = nodes // size
    half = slots // 2
    me = lax.axis_index("feat")

    asked_rank = ranks(asked)
    asked_count = jnp.sum(asked, axis=1)
    at = jnp.arange(STRIDE, dtype=I32)[None, :, None]
    chosen = (asked[:, None, :] > 0) & (asked_rank[:, None, :] == at)
    index = jnp.sum(jnp.where(chosen, jnp.arange(local, dtype=I32), 0), axis=2).reshape(-1)
    served = serve(features, index, asked_count, rows, capacity)
    panels = exchange(served).reshape(rows * capacity, width, size)

    far_tail = chip_swap(own_tiles[half:])
    tiles = (
        own_tiles,
        core_swap(own_tiles),
        far_head,
        far_tail,
        core_swap(far_head),
        core_swap(far_tail),
    )
    whole = ((0, 0, slots),), ((1, 0, slots),)
    lists = (
        feats,
        whole + (((2, 0, half), (3, half, half)), ((4, 0, half), (5, half, half))),
    )
    cotangents = gather_feat(cotangent)

    valid = code >= 0
    owner = jnp.where(valid, code >> 6, -1)
    block = jnp.where(valid, code & 63, -1)
    owner_hot = owner[:, None] == jnp.arange(rows, dtype=I32)[None, :]
    block_hot = block[:, None] == jnp.arange(local, dtype=I32)[None, :]
    slot_rank = jnp.sum(jnp.where(block_hot, exact_dot(owner_hot, rank), 0.0), axis=1).astype(I32)
    place = jnp.where(valid, owner * 64 + slot_rank, rows * 64)
    order = jnp.arange(feats * slots, dtype=I32)
    again = jnp.any(
        (code[:, None] == code[None, :]) & (order[None, :] < order[:, None]), axis=1
    ).astype(I32)
    counts = jnp.sum(valid.astype(I32).reshape(feats, slots), axis=1)

    own = aggregate(panels, tiles, lists, slots, place, target, counts, local, capacity)
    aggregated = gather_feat(own)
    activation, grads, weight_part = middle(weights, aggregated, cotangents)
    made = terms(grads, tiles, lists, slots, place, target, again, counts, rows, capacity)
    returned = exchange(made.reshape(rows, capacity * width, size))
    total = sum_rows(relative(weight_part, 1, me), rows)
    weight_grad = total * (1.0 / math.sqrt(nodes * rows))
    feature_grad = collect(returned, index, asked_count, local, width, capacity)
    return (activation, feature_grad, weight_grad)


def on_device(features, weight, cotangent, blocks, row_block, src_owner, src_block, live):
    rows = lax.axis_size("rows")
    feats = lax.axis_size("feat")
    me = lax.axis_index("feat")
    width, nodes = features.shape
    size = blocks.shape[2]
    slots = blocks.shape[1]
    local = nodes // size
    most = max(2, 2 * slots // rows) * feats

    own_tiles = blocks[0]
    far_head = chip_swap(own_tiles[: slots // 2])

    here = jnp.arange(slots, dtype=I32)
    alive = here < live[0, 0]
    code = jnp.where(alive, src_owner[0, :, 0] * 64 + src_block[0], -1)
    goal = jnp.where(alive, row_block[0], local)
    note = gather_feat(jnp.stack([code, goal]))
    code = jnp.concatenate([n[0] for n in note])
    target = jnp.concatenate([n[1] for n in note])
    valid = code >= 0
    owner = jnp.where(valid, code >> 6, -1)
    block = jnp.where(valid, code & 63, -1)
    owner_hot = owner[:, None] == jnp.arange(rows, dtype=I32)[None, :]
    block_hot = block[:, None] == jnp.arange(local, dtype=I32)[None, :]
    want = exact_dot(owner_hot.T, block_hot) > 0.5
    rank = ranks(want)
    largest = jnp.max(jnp.sum(want.astype(I32), axis=1))
    request = jnp.concatenate(
        [want.astype(I32), jnp.broadcast_to(largest, (rows, 128 - local))], axis=1
    )
    answer = exchange(request)
    asked = answer[:, :local]
    largest = jnp.max(answer[:, local])
    weights = relative(jnp.concatenate(gather_feat(weight), axis=0), 1, me)

    sizes = [c for c in CAPACITIES if c < most] + [most]
    which = jnp.sum((largest > jnp.asarray(sizes[:-1], I32)).astype(I32))
    return lax.switch(
        which,
        [functools.partial(body, c, rows, feats) for c in sizes],
        features,
        own_tiles,
        far_head,
        weights,
        cotangent,
        code,
        target,
        rank,
        asked,
    )


def solution(mesh):
    placed = (
        P("feat", "rows"),
        P("feat", None),
        P("feat", "rows"),
        P("rows", "feat", None, None),
        P("rows", "feat"),
        P("rows", "feat", None),
        P("rows", "feat"),
        P("rows", "feat"),
    )
    return jax.shard_map(
        on_device,
        mesh=mesh,
        in_specs=placed,
        out_specs=(P("feat", "rows"), P("feat", "rows"), P("feat", None)),
        check_vma=False,
    )
```

```python
import functools
import math

import jax
import jax.numpy as jnp
from jax import lax
from jax.experimental import pallas as pl
from jax.experimental.pallas import tpu as pltpu
from jax.sharding import PartitionSpec as P

BF = jnp.bfloat16
F32 = jnp.float32
I32 = jnp.int32
VMEM_LIMIT = 56 * 1024 * 1024
GROUP = 8
STRIDE = 16
UNROLL = 7
EDGE = 32
EXTRA = 2
HEAD = 40


def params():
    return pltpu.CompilerParams(vmem_limit_bytes=VMEM_LIMIT)


def core_swap(x):
    return lax.ppermute(x, "feat", [(0, 1), (1, 0), (2, 3), (3, 2)])


def chip_swap(x):
    return lax.ppermute(x, "feat", [(0, 2), (2, 0), (1, 3), (3, 1)])


def gather_feat(x):
    far = chip_swap(x)
    return (x, core_swap(x), far, core_swap(far))


def relative(x, axis, me):
    a = jnp.split(x, 4, axis=axis)
    low = (me & 1) == 1
    high = (me & 2) == 2
    b = [jnp.where(low, a[i ^ 1], a[i]) for i in range(4)]
    c = [jnp.where(high, b[i ^ 2], b[i]) for i in range(4)]
    return jnp.concatenate(c, axis=axis)


def exact_dot(a, b):
    return jnp.dot(a.astype(BF), b.astype(BF), preferred_element_type=F32)


def ranks(want):
    n = want.shape[-1]
    upper = jnp.arange(n)[:, None] < jnp.arange(n)[None, :]
    return exact_dot(want, upper).astype(I32)


def serve_kernel(step, main, index, count, features, out, over):
    width = features.shape[0]
    for i in range(step):
        row = pl.program_id(0) * step + i

        def put(ref, first, k):
            block = jnp.minimum(index[row, k], features.shape[1] // 128 - 1)
            start = pl.multiple_of(block * 128, 128)
            to = pl.multiple_of((k - first) * width, width)
            ref[i, pl.ds(to, width), :] = features[:, pl.ds(start, 128)]

        def body(g, carry):
            for u in range(UNROLL):
                put(out, 0, g * UNROLL + u)
            return carry

        lax.fori_loop(0, (jnp.minimum(count[row], main) + UNROLL - 1) // UNROLL, body, 0)

        @pl.when(count[row] > main)
        def _():
            for k in range(main, main + over.shape[1] // width):
                put(over, main, k)


def serve(features, index, count, rows, main, extra):
    width, nodes = features.shape
    step = 4
    place = lambda r, *_: (r, 0, 0)
    return pl.pallas_call(
        functools.partial(serve_kernel, step, main),
        grid_spec=pltpu.PrefetchScalarGridSpec(
            num_scalar_prefetch=2,
            grid=(rows // step,),
            in_specs=[pl.BlockSpec((width, nodes), lambda r, *_: (0, 0))],
            out_specs=[
                pl.BlockSpec((step, main * width, 128), place),
                pl.BlockSpec((step, extra * width, 128), place),
            ],
        ),
        out_shape=[
            jax.ShapeDtypeStruct((rows, main * width, 128), BF),
            jax.ShapeDtypeStruct((rows, extra * width, 128), BF),
        ],
        compiler_params=params(),
        cost_estimate=pl.CostEstimate(
            flops=0, bytes_accessed=rows * (main + extra) * width * 256, transcendentals=0
        ),
    )(index, count, features)


def tile_copies(lists, tiles, held, sems):
    copies, n = [], 0
    for j in range(lists[0]):
        group = []
        for piece, start, size in lists[1][j]:
            group.append(
                pltpu.make_async_copy(
                    tiles[piece], held.at[j, pl.ds(start, size)], sems.at[n]
                )
            )
            n += 1
        copies.append(group)
    return copies


def aggregate_kernel(lists, slots, place, target, live, flag, panels, over, *refs):
    pieces = sum(len(x) for x in lists[1])
    tiles = refs[:pieces]
    out, held, panel, acc, sems = refs[pieces:]
    blocks = out.shape[0]
    rows, main = panels.shape[:2]
    extra = over.shape[1]
    first = pltpu.make_async_copy(panels, panel.at[pl.ds(0, rows), pl.ds(0, main)], sems.at[pieces])
    first.start()
    copies = tile_copies(lists, tiles, held, sems)
    for group in copies:
        for c in group:
            c.start()
    acc[...] = jnp.zeros_like(acc)

    @pl.when(flag[0] > 0)
    def _():
        more = pltpu.make_async_copy(
            over, panel.at[pl.ds(0, rows), pl.ds(main, extra)], sems.at[pieces + 1]
        )
        more.start()
        more.wait()

    first.wait()
    for j in range(lists[0]):
        for c in copies[j]:
            c.wait()

        def body(g, carry, j=j):
            base = g * GROUP
            products = []
            for u in range(GROUP):
                s = j * slots + base + u
                products.append(
                    lax.dot_general(
                        panel[place[s] >> 6, place[s] & 63],
                        held[j, base + u],
                        (((1,), (1,)), ((), ())),
                        preferred_element_type=F32,
                    )
                )
            for u in range(GROUP):
                t = target[j * slots + base + u]
                acc[t] = acc[t] + products[u]
            return carry

        lax.fori_loop(0, (live[j] + GROUP - 1) // GROUP, body, 0)
    out[...] = acc[:blocks].astype(BF)


def aggregate(panels, over, tiles, lists, slots, place, target, live, flag, blocks):
    size = tiles[0].shape[1]
    rows, main, width, _ = panels.shape
    extra = over.shape[1]
    any_spec = pl.BlockSpec(memory_space=pl.ANY)
    return pl.pallas_call(
        functools.partial(aggregate_kernel, lists, slots),
        grid_spec=pltpu.PrefetchScalarGridSpec(
            num_scalar_prefetch=4,
            grid=(1,),
            in_specs=[any_spec] * (len(tiles) + 2),
            out_specs=pl.BlockSpec((blocks, width, size), lambda i, *_: (0, 0, 0)),
            scratch_shapes=[
                pltpu.VMEM((lists[0], slots, size, size), BF),
                pltpu.VMEM((rows + 1, main + extra, width, size), BF),
                pltpu.VMEM((blocks + 1, width, size), F32),
                pltpu.SemaphoreType.DMA((len(tiles) + 2,)),
            ],
        ),
        out_shape=jax.ShapeDtypeStruct((blocks, width, size), BF),
        compiler_params=params(),
        cost_estimate=pl.CostEstimate(
            flops=2 * lists[0] * slots * width * size * size,
            bytes_accessed=rows * main * width * size * 2 + lists[0] * slots * size * size * 2,
            transcendentals=0,
        ),
    )(place, target, live, flag, panels, over, *tiles)


def middle_kernel(step, weight, a0, a1, a2, a3, c0, c1, c2, c3, act, grad, wgrad, wsum):
    width = a0.shape[1]
    x = jnp.concatenate(
        [jnp.concatenate([a[b] for b in range(step)], axis=1) for a in (a0, a1, a2, a3)], axis=0
    )
    w = weight[...]
    preact = jnp.dot(w, x, preferred_element_type=F32)
    positive = jnp.maximum(preact, 0.0)
    own = positive[:width]
    act[...] = (own * own).astype(BF)
    cot = jnp.concatenate([c[...] for c in (c0, c1, c2, c3)], axis=0)
    pre = (2.0 * cot.astype(F32) * positive).astype(BF)
    g = lax.dot_general(
        w[:, :width], pre, (((0,), (0,)), ((), ())), preferred_element_type=F32
    ).astype(BF)
    for b in range(step):
        grad[b] = g[:, b * 128 : (b + 1) * 128]
    part = lax.dot_general(
        pre[:width], x, (((1,), (1,)), ((), ())), preferred_element_type=F32
    )

    @pl.when(pl.program_id(0) == 0)
    def _():
        wsum[...] = part

    @pl.when(pl.program_id(0) > 0)
    def _():
        wsum[...] = wsum[...] + part

    @pl.when(pl.program_id(0) == pl.num_programs(0) - 1)
    def _():
        for h in range(part.shape[1] // 128):
            wgrad[h * width : (h + 1) * width, :] = wsum[:, h * 128 : (h + 1) * 128].astype(BF)


def middle(weight, aggregated, cotangent):
    blocks, width, size = aggregated[0].shape
    hidden = weight.shape[0]
    step = 8 if blocks % 8 == 0 else 1
    a_spec = pl.BlockSpec((step, width, size), lambda i: (i, 0, 0))
    c_spec = pl.BlockSpec((width, step * size), lambda i: (0, i))
    tall = width * hidden // 128
    w_spec = pl.BlockSpec((tall, 128), lambda i: (0, 0))
    return pl.pallas_call(
        functools.partial(middle_kernel, step),
        grid=(blocks // step,),
        in_specs=[pl.BlockSpec((hidden, hidden), lambda i: (0, 0))] + [a_spec] * 4 + [c_spec] * 4,
        out_specs=[c_spec, a_spec, w_spec],
        out_shape=[
            jax.ShapeDtypeStruct((width, blocks * size), BF),
            jax.ShapeDtypeStruct((blocks, width, size), BF),
            jax.ShapeDtypeStruct((tall, 128), BF),
        ],
        scratch_shapes=[pltpu.VMEM((width, hidden), F32)],
        compiler_params=params(),
        cost_estimate=pl.CostEstimate(
            flops=2 * hidden * (hidden + 2 * width) * blocks * size,
            bytes_accessed=10 * blocks * width * size * 2,
            transcendentals=0,
        ),
    )(weight, *aggregated, *cotangent)


def terms_kernel(lists, slots, place, target, again, live, grads, shares, *refs):
    pieces = sum(len(x) for x in lists[1])
    tiles = refs[:pieces]
    out, over, held, made, sems = refs[pieces:]
    rows, tall = out.shape[:2]
    extra = over.shape[1]
    width = grads.shape[1]
    copies = tile_copies(lists, tiles, held, sems)
    for group in copies:
        for c in group:
            c.start()
    for r in range(rows):
        h = r % (shares.shape[0] // EDGE)
        made[r, :EDGE, :] = shares[h * EDGE : (h + 1) * EDGE, :]
    for j in range(lists[0]):
        for c in copies[j]:
            c.wait()

        def body(g, carry, j=j):
            base = g * GROUP
            products = []
            for u in range(GROUP):
                s = j * slots + base + u
                t = jnp.minimum(target[s], grads.shape[0] - 1)
                products.append(
                    jnp.dot(grads[t], held[j, base + u], preferred_element_type=F32)
                )
            for u in range(GROUP):
                s = j * slots + base + u
                at = pl.ds(pl.multiple_of(EDGE + (place[s] & 63) * width, EDGE), width)
                p = place[s] >> 6
                kept = jnp.where(again[s] > 0, made[p, at, :].astype(F32), 0.0)
                made[p, at, :] = (kept + products[u]).astype(BF)
            return carry

        lax.fori_loop(0, (live[j] + GROUP - 1) // GROUP, body, 0)
    last = [
        pltpu.make_async_copy(made.at[pl.ds(0, rows), pl.ds(0, tall)], out, sems.at[pieces]),
        pltpu.make_async_copy(
            made.at[pl.ds(0, rows), pl.ds(tall, extra)], over, sems.at[pieces + 1]
        ),
    ]
    for c in last:
        c.start()
    for c in last:
        c.wait()


def terms(grads, shares, tiles, lists, slots, place, target, again, live, rows, main, extra):
    size = tiles[0].shape[1]
    blocks, width, _ = grads.shape
    any_spec = pl.BlockSpec(memory_space=pl.ANY)
    return pl.pallas_call(
        functools.partial(terms_kernel, lists, slots),
        grid_spec=pltpu.PrefetchScalarGridSpec(
            num_scalar_prefetch=4,
            grid=(1,),
            in_specs=[
                pl.BlockSpec((blocks, width, size), lambda i, *_: (0, 0, 0)),
                pl.BlockSpec(shares.shape, lambda i, *_: (0, 0)),
            ]
            + [any_spec] * len(tiles),
            out_specs=[any_spec, any_spec],
            scratch_shapes=[
                pltpu.VMEM((lists[0], slots, size, size), BF),
                pltpu.VMEM((rows + 1, EDGE + (main + extra) * width, size), BF),
                pltpu.SemaphoreType.DMA((len(tiles) + 2,)),
            ],
        ),
        out_shape=[
            jax.ShapeDtypeStruct((rows, EDGE + main * width, size), BF),
            jax.ShapeDtypeStruct((rows, extra * width, size), BF),
        ],
        compiler_params=params(),
        cost_estimate=pl.CostEstimate(
            flops=2 * lists[0] * slots * width * size * size,
            bytes_accessed=rows * main * width * size * 2 + lists[0] * slots * size * size * 2,
            transcendentals=0,
        ),
    )(place, target, again, live, grads, shares, *tiles)


def collect_kernel(step, blocks, main, index, count, incoming, over, out, acc):
    width = out.shape[0]

    @pl.when(pl.program_id(0) == 0)
    def _():
        acc[...] = jnp.zeros_like(acc)

    for i in range(step):
        row = pl.program_id(0) * step + i

        def add(ref, shift, k):
            t = index[row, k]
            start = pl.multiple_of(k * width + shift, EDGE)
            acc[t] = acc[t] + ref[i, pl.ds(start, width), :].astype(F32)

        def body(g, carry):
            for u in range(UNROLL):
                add(incoming, EDGE, g * UNROLL + u)
            return carry

        lax.fori_loop(0, (jnp.minimum(count[row], main) + UNROLL - 1) // UNROLL, body, 0)

        @pl.when(count[row] > main)
        def _():
            for k in range(main, main + over.shape[1] // width):
                add(over, -main * width, k)

    @pl.when(pl.program_id(0) == pl.num_programs(0) - 1)
    def _():
        for b in range(blocks):
            out[:, b * 128 : (b + 1) * 128] = acc[b].astype(BF)


def collect(incoming, over, index, count, blocks, width, main, extra):
    rows = incoming.shape[0]
    step = 4
    place = lambda r, *_: (r, 0, 0)
    return pl.pallas_call(
        functools.partial(collect_kernel, step, blocks, main),
        grid_spec=pltpu.PrefetchScalarGridSpec(
            num_scalar_prefetch=2,
            grid=(rows // step,),
            in_specs=[
                pl.BlockSpec((step, EDGE + main * width, 128), place),
                pl.BlockSpec((step, extra * width, 128), place),
            ],
            out_specs=pl.BlockSpec((width, blocks * 128), lambda r, *_: (0, 0)),
            scratch_shapes=[pltpu.VMEM((blocks + 1, width, 128), F32)],
        ),
        out_shape=jax.ShapeDtypeStruct((width, blocks * 128), BF),
        compiler_params=params(),
        cost_estimate=pl.CostEstimate(
            flops=rows * main * width * 128,
            bytes_accessed=rows * main * width * 256,
            transcendentals=0,
        ),
    )(index, count, incoming, over)


def exchange(x):
    return lax.all_to_all(x, "rows", split_axis=0, concat_axis=0, tiled=True)


def exchange_both(main, over, needed):
    over = lax.cond(needed, exchange, lambda x: x, over)
    main, over = lax.optimization_barrier((main, over))
    return exchange(main), over


def share_total_kernel(incoming, out):
    total = incoming[0].astype(F32)
    for r in range(1, incoming.shape[0]):
        total = total + incoming[r].astype(F32)
    out[...] = total


def share_total(returned):
    rows = returned.shape[0]
    return pl.pallas_call(
        share_total_kernel,
        grid=(1,),
        in_specs=[pl.BlockSpec((rows, EDGE, 128), lambda i: (0, 0, 0))],
        out_specs=pl.BlockSpec((EDGE, 128), lambda i: (0, 0)),
        out_shape=jax.ShapeDtypeStruct((EDGE, 128), F32),
        compiler_params=params(),
    )(returned)


def share_sum(piece, parts, rows):
    row = lax.axis_index("rows")
    have = [piece] + [
        lax.ppermute(piece, "rows", [(i, i ^ k) for i in range(rows)]) for k in range(1, parts)
    ]
    bit = 1
    while bit < parts:
        odd = (row & bit) > 0
        have = [jnp.where(odd, have[i ^ bit], have[i]) for i in range(parts)]
        bit *= 2
    return have


def on_device(features, weight, cotangent, blocks, row_block, src_owner, src_block, live):
    rows = lax.axis_size("rows")
    feats = lax.axis_size("feat")
    me = lax.axis_index("feat")
    width, nodes = features.shape
    size = blocks.shape[2]
    slots = blocks.shape[1]
    local = nodes // size
    most = max(2, 2 * slots // rows) * feats
    extra = EXTRA
    main = most - extra
    head = HEAD

    own_tiles = blocks[0]
    far_head = chip_swap(own_tiles[:head])

    here = jnp.arange(slots, dtype=I32)
    alive = here < live[0, 0]
    code = jnp.where(alive, src_owner[0, :, 0] * 64 + src_block[0], -1)
    goal = jnp.where(alive, row_block[0], local)
    note = gather_feat(jnp.stack([code, goal]))
    code = jnp.concatenate([n[0] for n in note])
    target = jnp.concatenate([n[1] for n in note])
    valid = code >= 0
    owner = jnp.where(valid, code >> 6, -1)
    block = jnp.where(valid, code & 63, -1)
    owner_hot = owner[:, None] == jnp.arange(rows, dtype=I32)[None, :]
    block_hot = block[:, None] == jnp.arange(local, dtype=I32)[None, :]
    want = exact_dot(owner_hot.T, block_hot) > 0.5
    rank = ranks(want)
    largest = jnp.max(jnp.sum(want.astype(I32), axis=1))
    request = jnp.concatenate(
        [want.astype(I32), jnp.broadcast_to(largest, (rows, 128 - local))], axis=1
    )
    weights = relative(jnp.concatenate(gather_feat(weight), axis=0), 1, me)

    slot_rank = jnp.sum(jnp.where(block_hot, exact_dot(owner_hot, rank), 0.0), axis=1).astype(I32)
    place = jnp.where(valid, owner * 64 + slot_rank, rows * 64)
    order = jnp.arange(feats * slots, dtype=I32)
    again = jnp.any(
        (code[:, None] == code[None, :]) & (order[None, :] < order[:, None]), axis=1
    ).astype(I32)
    counts = jnp.sum(valid.astype(I32).reshape(feats, slots), axis=1)
    answer = exchange(request)
    answer, far_head, weights, place, again, counts, target = lax.optimization_barrier(
        (answer, far_head, weights, place, again, counts, target)
    )
    asked = answer[:, :local]
    needed = jnp.max(answer[:, local]) > main
    asked_rank = ranks(asked)
    asked_count = jnp.sum(asked, axis=1)
    at = jnp.arange(STRIDE, dtype=I32)[None, :, None]
    chosen = (asked[:, None, :] > 0) & (asked_rank[:, None, :] == at)
    index = local + jnp.sum(jnp.where(chosen, jnp.arange(local, dtype=I32) - local, 0), axis=2)
    served, over = serve(features, index, asked_count, rows, main, extra)
    panels, over = exchange_both(served, over, needed)
    panels = panels.reshape(rows, main, width, size)
    over = over.reshape(rows, extra, width, size)

    far_tail, cotangent, answer = lax.optimization_barrier((own_tiles[head:], cotangent, answer))
    far_tail = chip_swap(far_tail)
    tiles = (
        own_tiles,
        core_swap(own_tiles),
        far_head,
        far_tail,
        core_swap(far_head),
        core_swap(far_tail),
    )
    lists = (
        feats,
        (
            ((0, 0, slots),),
            ((1, 0, slots),),
            ((2, 0, head), (3, head, slots - head)),
            ((4, 0, head), (5, head, slots - head)),
        ),
    )
    cotangents = gather_feat(cotangent)
    flag = needed.astype(I32).reshape(1)

    own = aggregate(panels, over, tiles, lists, slots, place, target, counts, flag, local)
    aggregated = gather_feat(own)
    activation, grads, shares = middle(weights, aggregated, cotangents)
    made, over = terms(
        grads, shares, tiles, lists, slots, place, target, again, counts, rows, main, extra
    )
    returned, over = exchange_both(made, over, needed)
    piece = share_total(returned)
    total = jnp.concatenate(share_sum(piece, shares.shape[0] // EDGE, rows), axis=0)
    total = jnp.concatenate(jnp.split(total, total.shape[0] // width, axis=0), axis=1)
    weight_grad = relative(total, 1, me) * (1.0 / math.sqrt(nodes * rows))
    feature_grad = collect(returned, over, index, asked_count, local, width, main, extra)
    return (activation, feature_grad, weight_grad)


def solution(mesh):
    placed = (
        P("feat", "rows"),
        P("feat", None),
        P("feat", "rows"),
        P("rows", "feat", None, None),
        P("rows", "feat"),
        P("rows", "feat", None),
        P("rows", "feat"),
        P("rows", "feat"),
    )
    return jax.shard_map(
        on_device,
        mesh=mesh,
        in_specs=placed,
        out_specs=(P("feat", "rows"), P("feat", "rows"), P("feat", None)),
        check_vma=False,
    )
```

```python
import functools
import math

import jax
import jax.numpy as jnp
from jax import lax
from jax.experimental import pallas as pl
from jax.experimental.pallas import tpu as pltpu
from jax.sharding import PartitionSpec as P

BF = jnp.bfloat16
F32 = jnp.float32
I32 = jnp.int32
VMEM_LIMIT = 56 * 1024 * 1024
GROUP = 8
STRIDE = 16
EDGE = 32
EXTRA = 2
HEAD = 40


def params():
    return pltpu.CompilerParams(vmem_limit_bytes=VMEM_LIMIT)


def core_swap(x):
    return lax.ppermute(x, "feat", [(0, 1), (1, 0), (2, 3), (3, 2)])


def chip_swap(x):
    return lax.ppermute(x, "feat", [(0, 2), (2, 0), (1, 3), (3, 1)])


def gather_feat(x):
    far = chip_swap(x)
    return (x, core_swap(x), far, core_swap(far))


def relative(x, axis, me):
    a = jnp.split(x, 4, axis=axis)
    low = (me & 1) == 1
    high = (me & 2) == 2
    b = [jnp.where(low, a[i ^ 1], a[i]) for i in range(4)]
    c = [jnp.where(high, b[i ^ 2], b[i]) for i in range(4)]
    return jnp.concatenate(c, axis=axis)


def exact_dot(a, b):
    return jnp.dot(a.astype(BF), b.astype(BF), preferred_element_type=F32)


def ranks(want):
    n = want.shape[-1]
    upper = jnp.arange(n)[:, None] < jnp.arange(n)[None, :]
    return exact_dot(want, upper).astype(I32)


def each_row(rows, first, act):
    def body(r, carry):
        act(r)
        return carry

    lax.fori_loop(first, rows, body, 0)


def serve_kernel(spans, index, count, features, out, over, buf, sems):
    width = features.shape[0]
    rows = out.shape[0]
    main = spans[-1][0]

    def sent(r, n):
        low, high = spans[n]
        ref, base = (over, main) if low >= main else (out, 0)
        return pltpu.make_async_copy(
            buf.at[r, pl.ds(low * width, (high - low) * width)],
            ref.at[r, pl.ds((low - base) * width, (high - low) * width)],
            sems.at[r, n],
        )

    def fill(r, n):
        for k in range(*spans[n]):
            block = jnp.minimum(index[r, k], features.shape[1] // 128 - 1)
            start = pl.multiple_of(block * 128, 128)
            buf[r, k * width : (k + 1) * width, :] = features[:, pl.ds(start, 128)]
        sent(r, n).start()

    def spread(act):
        def body(r):
            act(r, 0)
            for n in (1, 2):
                pl.when(count[r] > spans[n][0])(functools.partial(act, r, n))

        each_row(rows, 0, body)

    spread(fill)
    spread(lambda r, n: sent(r, n).wait())


def serve(features, index, count, rows, main, extra):
    width, nodes = features.shape
    any_spec = pl.BlockSpec(memory_space=pl.ANY)
    spans = ((0, main // 2), (main // 2, main), (main, main + extra))
    return pl.pallas_call(
        functools.partial(serve_kernel, spans),
        grid_spec=pltpu.PrefetchScalarGridSpec(
            num_scalar_prefetch=2,
            grid=(1,),
            in_specs=[pl.BlockSpec((width, nodes), lambda r, *_: (0, 0))],
            out_specs=[any_spec, any_spec],
            scratch_shapes=[
                pltpu.VMEM((rows, (main + extra) * width, 128), BF),
                pltpu.SemaphoreType.DMA((rows, 3)),
            ],
        ),
        out_shape=[
            jax.ShapeDtypeStruct((rows, main * width, 128), BF),
            jax.ShapeDtypeStruct((rows, extra * width, 128), BF),
        ],
        compiler_params=params(),
        cost_estimate=pl.CostEstimate(
            flops=0, bytes_accessed=rows * (main + extra) * width * 256, transcendentals=0
        ),
    )(index, count, features)


def tile_copies(lists, tiles, held, sems):
    copies, n = [], 0
    for j in range(lists[0]):
        group = []
        for piece, start, size in lists[1][j]:
            group.append(
                pltpu.make_async_copy(
                    tiles[piece], held.at[j, pl.ds(start, size)], sems.at[n]
                )
            )
            n += 1
        copies.append(group)
    return copies


def aggregate_kernel(lists, slots, place, target, live, used, panels, over, *refs):
    pieces = sum(len(x) for x in lists[1])
    tiles = refs[:pieces]
    out, held, panel, acc, sems, row_sems = refs[pieces:]
    blocks = out.shape[0]
    rows, main = panels.shape[:2]
    extra = over.shape[1]
    half = main // 2
    first = pltpu.make_async_copy(
        panels.at[:, pl.ds(0, half)], panel.at[pl.ds(0, rows), pl.ds(0, half)], sems.at[pieces]
    )
    first.start()

    def late(r):
        return pltpu.make_async_copy(
            panels.at[r, pl.ds(half, main - half)],
            panel.at[r, pl.ds(half, main - half)],
            row_sems.at[r, 0],
        )

    def more(r):
        return pltpu.make_async_copy(over.at[r], panel.at[r, pl.ds(main, extra)], row_sems.at[r, 1])

    def start(r):
        pl.when(used[r] > half)(lambda: late(r).start())
        pl.when(used[r] > main)(lambda: more(r).start())

    def finish(r):
        pl.when(used[r] > half)(lambda: late(r).wait())
        pl.when(used[r] > main)(lambda: more(r).wait())

    each_row(rows, 0, start)
    copies = tile_copies(lists, tiles, held, sems)
    for group in copies:
        for c in group:
            c.start()
    acc[...] = jnp.zeros_like(acc)

    each_row(rows, 0, finish)
    first.wait()
    for j in range(lists[0]):
        for c in copies[j]:
            c.wait()

        def body(g, carry, j=j):
            base = g * GROUP
            products = []
            for u in range(GROUP):
                s = j * slots + base + u
                products.append(
                    lax.dot_general(
                        panel[place[s] >> 6, place[s] & 63],
                        held[j, base + u],
                        (((1,), (1,)), ((), ())),
                        preferred_element_type=F32,
                    )
                )
            for u in range(GROUP):
                t = target[j * slots + base + u]
                acc[u % 2, t] = acc[u % 2, t] + products[u]
            return carry

        lax.fori_loop(0, (live[j] + GROUP - 1) // GROUP, body, 0)
    for t in range(blocks):
        out[t] = (acc[0, t] + acc[1, t]).astype(BF)


def aggregate(panels, over, tiles, lists, slots, place, target, live, used, blocks):
    size = tiles[0].shape[1]
    rows, main, width, _ = panels.shape
    extra = over.shape[1]
    any_spec = pl.BlockSpec(memory_space=pl.ANY)
    return pl.pallas_call(
        functools.partial(aggregate_kernel, lists, slots),
        grid_spec=pltpu.PrefetchScalarGridSpec(
            num_scalar_prefetch=4,
            grid=(1,),
            in_specs=[any_spec] * (len(tiles) + 2),
            out_specs=pl.BlockSpec((blocks, width, size), lambda i, *_: (0, 0, 0)),
            scratch_shapes=[
                pltpu.VMEM((lists[0], slots, size, size), BF),
                pltpu.VMEM((rows + 1, main + extra, width, size), BF),
                pltpu.VMEM((2, blocks + 1, width, size), F32),
                pltpu.SemaphoreType.DMA((len(tiles) + 1,)),
                pltpu.SemaphoreType.DMA((rows, 2)),
            ],
        ),
        out_shape=jax.ShapeDtypeStruct((blocks, width, size), BF),
        compiler_params=params(),
        cost_estimate=pl.CostEstimate(
            flops=2 * lists[0] * slots * width * size * size,
            bytes_accessed=rows * main * width * size * 2 + lists[0] * slots * size * size * 2,
            transcendentals=0,
        ),
    )(place, target, live, used, panels, over, *tiles)


def middle_kernel(step, weight, a0, a1, a2, a3, c0, c1, c2, c3, act, grad, wgrad, wsum):
    width = a0.shape[1]
    x = jnp.concatenate(
        [jnp.concatenate([a[b] for b in range(step)], axis=1) for a in (a0, a1, a2, a3)], axis=0
    )
    w = weight[...]
    preact = jnp.dot(w, x, preferred_element_type=F32)
    positive = jnp.maximum(preact, 0.0)
    own = positive[:width]
    act[...] = (own * own).astype(BF)
    cot = jnp.concatenate([c[...] for c in (c0, c1, c2, c3)], axis=0)
    pre = (2.0 * cot.astype(F32) * positive).astype(BF)
    g = lax.dot_general(
        w[:, :width], pre, (((0,), (0,)), ((), ())), preferred_element_type=F32
    ).astype(BF)
    for b in range(step):
        grad[b] = g[:, b * 128 : (b + 1) * 128]
    part = lax.dot_general(
        pre[:width], x, (((1,), (1,)), ((), ())), preferred_element_type=F32
    )

    @pl.when(pl.program_id(0) == 0)
    def _():
        wsum[...] = part

    @pl.when(pl.program_id(0) > 0)
    def _():
        wsum[...] = wsum[...] + part

    @pl.when(pl.program_id(0) == pl.num_programs(0) - 1)
    def _():
        for h in range(part.shape[1] // 128):
            wgrad[h * width : (h + 1) * width, :] = wsum[:, h * 128 : (h + 1) * 128].astype(BF)


def middle(weight, aggregated, cotangent):
    blocks, width, size = aggregated[0].shape
    hidden = weight.shape[0]
    step = 8 if blocks % 8 == 0 else 1
    a_spec = pl.BlockSpec((step, width, size), lambda i: (i, 0, 0))
    c_spec = pl.BlockSpec((width, step * size), lambda i: (0, i))
    tall = width * hidden // 128
    w_spec = pl.BlockSpec((tall, 128), lambda i: (0, 0))
    return pl.pallas_call(
        functools.partial(middle_kernel, step),
        grid=(blocks // step,),
        in_specs=[pl.BlockSpec((hidden, hidden), lambda i: (0, 0))] + [a_spec] * 4 + [c_spec] * 4,
        out_specs=[c_spec, a_spec, w_spec],
        out_shape=[
            jax.ShapeDtypeStruct((width, blocks * size), BF),
            jax.ShapeDtypeStruct((blocks, width, size), BF),
            jax.ShapeDtypeStruct((tall, 128), BF),
        ],
        scratch_shapes=[pltpu.VMEM((width, hidden), F32)],
        compiler_params=params(),
        cost_estimate=pl.CostEstimate(
            flops=2 * hidden * (hidden + 2 * width) * blocks * size,
            bytes_accessed=10 * blocks * width * size * 2,
            transcendentals=0,
        ),
    )(weight, *aggregated, *cotangent)


def terms_kernel(lists, slots, half, place, target, again, live, used, grads, shares, *refs):
    pieces = sum(len(x) for x in lists[1])
    tiles = refs[:pieces]
    out, over, held, made, sems, row_sems = refs[pieces:]
    rows, tall = out.shape[:2]
    extra = over.shape[1]
    width = grads.shape[1]
    copies = tile_copies(lists, tiles, held, sems)
    for group in copies:
        for c in group:
            c.start()
    for r in range(rows):
        h = r % (shares.shape[0] // EDGE)
        made[r, :EDGE, :] = shares[h * EDGE : (h + 1) * EDGE, :]
    for j in range(lists[0]):
        for c in copies[j]:
            c.wait()

        def body(g, carry, j=j):
            base = g * GROUP
            products = []
            for u in range(GROUP):
                s = j * slots + base + u
                t = jnp.minimum(target[s], grads.shape[0] - 1)
                products.append(
                    jnp.dot(grads[t], held[j, base + u], preferred_element_type=F32)
                )
            plain = again[j * slots + base]
            for u in range(1, GROUP):
                plain = plain + again[j * slots + base + u]

            def put(u, keep):
                s = j * slots + base + u
                at = pl.ds(pl.multiple_of(EDGE + (place[s] & 63) * width, EDGE), width)
                p = place[s] >> 6
                value = products[u]
                if keep:
                    value = value + jnp.where(again[s] > 0, made[p, at, :].astype(F32), 0.0)
                made[p, at, :] = value.astype(BF)

            @pl.when(plain == 0)
            def _():
                for u in range(GROUP):
                    put(u, False)

            @pl.when(plain > 0)
            def _():
                for u in range(GROUP):
                    put(u, True)

            return carry

        lax.fori_loop(0, (live[j] + GROUP - 1) // GROUP, body, 0)
    first = EDGE + half * width
    whole = pltpu.make_async_copy(
        made.at[pl.ds(0, rows), pl.ds(0, first)], out.at[:, pl.ds(0, first)], sems.at[pieces]
    )
    whole.start()

    def late(r):
        span = pl.ds(first, tall - first)
        return pltpu.make_async_copy(made.at[r, span], out.at[r, span], row_sems.at[r, 0])

    def more(r):
        return pltpu.make_async_copy(made.at[r, pl.ds(tall, extra)], over.at[r], row_sems.at[r, 1])

    def start(r):
        pl.when(used[r] > half)(lambda: late(r).start())
        pl.when(used[r] > 2 * half)(lambda: more(r).start())

    def finish(r):
        pl.when(used[r] > half)(lambda: late(r).wait())
        pl.when(used[r] > 2 * half)(lambda: more(r).wait())

    each_row(rows, 0, start)
    each_row(rows, 0, finish)
    whole.wait()


def terms(grads, shares, tiles, lists, slots, place, target, again, live, used, rows, main, extra):
    size = tiles[0].shape[1]
    blocks, width, _ = grads.shape
    any_spec = pl.BlockSpec(memory_space=pl.ANY)
    return pl.pallas_call(
        functools.partial(terms_kernel, lists, slots, main // 2),
        grid_spec=pltpu.PrefetchScalarGridSpec(
            num_scalar_prefetch=5,
            grid=(1,),
            in_specs=[
                pl.BlockSpec((blocks, width, size), lambda i, *_: (0, 0, 0)),
                pl.BlockSpec(shares.shape, lambda i, *_: (0, 0)),
            ]
            + [any_spec] * len(tiles),
            out_specs=[any_spec, any_spec],
            scratch_shapes=[
                pltpu.VMEM((lists[0], slots, size, size), BF),
                pltpu.VMEM((rows + 1, EDGE + (main + extra) * width, size), BF),
                pltpu.SemaphoreType.DMA((len(tiles) + 1,)),
                pltpu.SemaphoreType.DMA((rows, 2)),
            ],
        ),
        out_shape=[
            jax.ShapeDtypeStruct((rows, EDGE + main * width, size), BF),
            jax.ShapeDtypeStruct((rows, extra * width, size), BF),
        ],
        compiler_params=params(),
        cost_estimate=pl.CostEstimate(
            flops=2 * lists[0] * slots * width * size * size,
            bytes_accessed=rows * main * width * size * 2 + lists[0] * slots * size * size * 2,
            transcendentals=0,
        ),
    )(place, target, again, live, used, grads, shares, *tiles)


def collect_kernel(chains, spans, blocks, index, count, incoming, over, out, buf, acc, sems):
    width = out.shape[0]
    rows = incoming.shape[0]
    main = spans[-1][0]

    def came(r, n):
        low, high = spans[n]
        if low >= main:
            source = over.at[r]
        else:
            source = incoming.at[r, pl.ds(EDGE + low * width, (high - low) * width)]
        return pltpu.make_async_copy(
            source, buf.at[r, pl.ds(low * width, (high - low) * width)], sems.at[r, n]
        )

    def spread(act, r):
        act(r, 0)
        for n in (1, 2):
            pl.when(count[r] > spans[n][0])(functools.partial(act, r, n))

    each_row(rows, 0, functools.partial(spread, lambda r, n: came(r, n).start()))
    acc[...] = jnp.zeros_like(acc)

    def add(g, n):
        for k in range(*spans[n]):
            for q in range(chains):
                r = g * chains + q
                t = index[r, k]
                acc[q, t] = acc[q, t] + buf[r, k * width : (k + 1) * width, :].astype(F32)

    def body(g):
        most = count[g * chains]
        for q in range(chains):
            spread(lambda r, n: came(r, n).wait(), g * chains + q)
            most = jnp.maximum(most, count[g * chains + q])
        add(g, 0)
        for n in (1, 2):
            pl.when(most > spans[n][0])(functools.partial(add, g, n))

    each_row(rows // chains, 0, body)
    for b in range(blocks):
        total = acc[0, b]
        for q in range(1, chains):
            total = total + acc[q, b]
        out[:, b * 128 : (b + 1) * 128] = total.astype(BF)


def collect(incoming, over, index, count, blocks, width, main, extra):
    rows = incoming.shape[0]
    chains = 4
    any_spec = pl.BlockSpec(memory_space=pl.ANY)
    spans = ((0, main // 2), (main // 2, main), (main, main + extra))
    return pl.pallas_call(
        functools.partial(collect_kernel, chains, spans, blocks),
        grid_spec=pltpu.PrefetchScalarGridSpec(
            num_scalar_prefetch=2,
            grid=(1,),
            in_specs=[any_spec, any_spec],
            out_specs=pl.BlockSpec((width, blocks * 128), lambda r, *_: (0, 0)),
            scratch_shapes=[
                pltpu.VMEM((rows, (main + extra) * width, 128), BF),
                pltpu.VMEM((chains, blocks + 1, width, 128), F32),
                pltpu.SemaphoreType.DMA((rows, 3)),
            ],
        ),
        out_shape=jax.ShapeDtypeStruct((width, blocks * 128), BF),
        compiler_params=params(),
        cost_estimate=pl.CostEstimate(
            flops=rows * main * width * 128,
            bytes_accessed=rows * main * width * 256,
            transcendentals=0,
        ),
    )(index, count, incoming, over)


def exchange(x):
    return lax.all_to_all(x, "rows", split_axis=0, concat_axis=0, tiled=True)


def exchange_both(main, over, needed):
    over = lax.cond(needed, exchange, lambda x: x, over)
    main, over = lax.optimization_barrier((main, over))
    return exchange(main), over


def share_total_kernel(incoming, out):
    total = incoming[0].astype(F32)
    for r in range(1, incoming.shape[0]):
        total = total + incoming[r].astype(F32)
    out[...] = total


def share_total(returned):
    rows = returned.shape[0]
    return pl.pallas_call(
        share_total_kernel,
        grid=(1,),
        in_specs=[pl.BlockSpec((rows, EDGE, 128), lambda i: (0, 0, 0))],
        out_specs=pl.BlockSpec((EDGE, 128), lambda i: (0, 0)),
        out_shape=jax.ShapeDtypeStruct((EDGE, 128), F32),
        compiler_params=params(),
    )(returned)


def share_sum(piece, parts, rows):
    row = lax.axis_index("rows")
    have = [piece] + [
        lax.ppermute(piece, "rows", [(i, i ^ k) for i in range(rows)]) for k in range(1, parts)
    ]
    bit = 1
    while bit < parts:
        odd = (row & bit) > 0
        have = [jnp.where(odd, have[i ^ bit], have[i]) for i in range(parts)]
        bit *= 2
    return have


def on_device(features, weight, cotangent, blocks, row_block, src_owner, src_block, live):
    rows = lax.axis_size("rows")
    feats = lax.axis_size("feat")
    me = lax.axis_index("feat")
    width, nodes = features.shape
    size = blocks.shape[2]
    slots = blocks.shape[1]
    local = nodes // size
    most = max(2, 2 * slots // rows) * feats
    extra = EXTRA
    main = most - extra
    head = HEAD

    own_tiles = blocks[0]
    far_head = chip_swap(own_tiles[:head])

    here = jnp.arange(slots, dtype=I32)
    alive = here < live[0, 0]
    code = jnp.where(alive, src_owner[0, :, 0] * 64 + src_block[0], -1)
    goal = jnp.where(alive, row_block[0], local)
    note = gather_feat(jnp.stack([code, goal]))
    code = jnp.concatenate([n[0] for n in note])
    target = jnp.concatenate([n[1] for n in note])
    valid = code >= 0
    owner = jnp.where(valid, code >> 6, -1)
    block = jnp.where(valid, code & 63, -1)
    owner_hot = owner[:, None] == jnp.arange(rows, dtype=I32)[None, :]
    block_hot = block[:, None] == jnp.arange(local, dtype=I32)[None, :]
    want = exact_dot(owner_hot.T, block_hot) > 0.5
    rank = ranks(want)
    used = jnp.sum(want.astype(I32), axis=1)
    largest = jnp.max(used)
    request = jnp.concatenate(
        [want.astype(I32), jnp.broadcast_to(largest, (rows, 128 - local))], axis=1
    )
    weights = relative(jnp.concatenate(gather_feat(weight), axis=0), 1, me)

    slot_rank = jnp.sum(jnp.where(block_hot, exact_dot(owner_hot, rank), 0.0), axis=1).astype(I32)
    place = jnp.where(valid, owner * 64 + slot_rank, rows * 64)
    order = jnp.arange(feats * slots, dtype=I32)
    again = jnp.any(
        (code[:, None] == code[None, :]) & (order[None, :] < order[:, None]), axis=1
    ).astype(I32)
    counts = jnp.sum(valid.astype(I32).reshape(feats, slots), axis=1)
    answer = exchange(request)
    answer, far_head, weights, place, again, counts, target = lax.optimization_barrier(
        (answer, far_head, weights, place, again, counts, target)
    )
    asked = answer[:, :local]
    needed = jnp.max(answer[:, local]) > main
    asked_rank = ranks(asked)
    asked_count = jnp.sum(asked, axis=1)
    at = jnp.arange(STRIDE, dtype=I32)[None, :, None]
    chosen = (asked[:, None, :] > 0) & (asked_rank[:, None, :] == at)
    index = local + jnp.sum(jnp.where(chosen, jnp.arange(local, dtype=I32) - local, 0), axis=2)
    served, over = serve(features, index, asked_count, rows, main, extra)
    panels, over = exchange_both(served, over, needed)
    panels = panels.reshape(rows, main, width, size)
    over = over.reshape(rows, extra, width, size)

    far_tail, cotangent, answer = lax.optimization_barrier((own_tiles[head:], cotangent, answer))
    far_tail = chip_swap(far_tail)
    tiles = (
        own_tiles,
        core_swap(own_tiles),
        far_head,
        far_tail,
        core_swap(far_head),
        core_swap(far_tail),
    )
    lists = (
        feats,
        (
            ((0, 0, slots),),
            ((1, 0, slots),),
            ((2, 0, head), (3, head, slots - head)),
            ((4, 0, head), (5, head, slots - head)),
        ),
    )
    cotangents = gather_feat(cotangent)

    own = aggregate(panels, over, tiles, lists, slots, place, target, counts, used, local)
    aggregated = gather_feat(own)
    activation, grads, shares = middle(weights, aggregated, cotangents)
    made, over = terms(
        grads, shares, tiles, lists, slots, place, target, again, counts, used, rows, main, extra
    )
    returned, over = exchange_both(made, over, needed)
    piece = share_total(returned)
    total = jnp.concatenate(share_sum(piece, shares.shape[0] // EDGE, rows), axis=0)
    total = jnp.concatenate(jnp.split(total, total.shape[0] // width, axis=0), axis=1)
    weight_grad = relative(total, 1, me) * (1.0 / math.sqrt(nodes * rows))
    feature_grad = collect(returned, over, index, asked_count, local, width, main, extra)
    return (activation, feature_grad, weight_grad)


def solution(mesh):
    placed = (
        P("feat", "rows"),
        P("feat", None),
        P("feat", "rows"),
        P("rows", "feat", None, None),
        P("rows", "feat"),
        P("rows", "feat", None),
        P("rows", "feat"),
        P("rows", "feat"),
    )
    return jax.shard_map(
        on_device,
        mesh=mesh,
        in_specs=placed,
        out_specs=(P("feat", "rows"), P("feat", "rows"), P("feat", None)),
        check_vma=False,
    )
```

```python
import functools
import math

import jax
import jax.numpy as jnp
from jax import lax
from jax.experimental import pallas as pl
from jax.experimental.pallas import tpu as pltpu
from jax.sharding import PartitionSpec as P

BF = jnp.bfloat16
F32 = jnp.float32
I32 = jnp.int32
VMEM_LIMIT = 56 * 1024 * 1024
GROUP = 8
STRIDE = 16
EDGE = 32
EXTRA = 2
HEAD = 40


def params():
    return pltpu.CompilerParams(vmem_limit_bytes=VMEM_LIMIT)


def core_swap(x):
    return lax.ppermute(x, "feat", [(0, 1), (1, 0), (2, 3), (3, 2)])


def chip_swap(x):
    return lax.ppermute(x, "feat", [(0, 2), (2, 0), (1, 3), (3, 1)])


def gather_feat(x):
    far = chip_swap(x)
    return (x, core_swap(x), far, core_swap(far))


def relative(x, axis, me):
    a = jnp.split(x, 4, axis=axis)
    low = (me & 1) == 1
    high = (me & 2) == 2
    b = [jnp.where(low, a[i ^ 1], a[i]) for i in range(4)]
    c = [jnp.where(high, b[i ^ 2], b[i]) for i in range(4)]
    return jnp.concatenate(c, axis=axis)


def exact_dot(a, b):
    return jnp.dot(a.astype(BF), b.astype(BF), preferred_element_type=F32)


def ranks(want):
    n = want.shape[-1]
    upper = jnp.arange(n)[:, None] < jnp.arange(n)[None, :]
    return exact_dot(want, upper).astype(I32)


def each_row(rows, first, act):
    def body(r, carry):
        act(r)
        return carry

    lax.fori_loop(first, rows, body, 0)


def serve_kernel(spans, index, count, features, out, over, buf, sems):
    width = features.shape[0]
    rows = out.shape[0]
    main = spans[-1][0]

    def sent(r, n):
        low, high = spans[n]
        ref, base = (over, main) if low >= main else (out, 0)
        return pltpu.make_async_copy(
            buf.at[r, pl.ds(low * width, (high - low) * width)],
            ref.at[r, pl.ds((low - base) * width, (high - low) * width)],
            sems.at[r, n],
        )

    def fill(r, n):
        for k in range(*spans[n]):
            block = jnp.minimum(index[r, k], features.shape[1] // 128 - 1)
            start = pl.multiple_of(block * 128, 128)
            buf[r, k * width : (k + 1) * width, :] = features[:, pl.ds(start, 128)]
        sent(r, n).start()

    def spread(act):
        def body(r):
            act(r, 0)
            for n in (1, 2):
                pl.when(count[r] > spans[n][0])(functools.partial(act, r, n))

        each_row(rows, 0, body)

    spread(fill)
    spread(lambda r, n: sent(r, n).wait())


def serve(features, index, count, rows, main, extra):
    width, nodes = features.shape
    any_spec = pl.BlockSpec(memory_space=pl.ANY)
    spans = ((0, main // 2), (main // 2, main), (main, main + extra))
    return pl.pallas_call(
        functools.partial(serve_kernel, spans),
        grid_spec=pltpu.PrefetchScalarGridSpec(
            num_scalar_prefetch=2,
            grid=(1,),
            in_specs=[pl.BlockSpec((width, nodes), lambda r, *_: (0, 0))],
            out_specs=[any_spec, any_spec],
            scratch_shapes=[
                pltpu.VMEM((rows, (main + extra) * width, 128), BF),
                pltpu.SemaphoreType.DMA((rows, 3)),
            ],
        ),
        out_shape=[
            jax.ShapeDtypeStruct((rows, main * width, 128), BF),
            jax.ShapeDtypeStruct((rows, extra * width, 128), BF),
        ],
        compiler_params=params(),
        cost_estimate=pl.CostEstimate(
            flops=0, bytes_accessed=rows * (main + extra) * width * 256, transcendentals=0
        ),
    )(index, count, features)


def tile_copies(lists, tiles, held, sems):
    copies, n = [], 0
    for j in range(lists[0]):
        group = []
        for piece, start, size in lists[1][j]:
            group.append(
                pltpu.make_async_copy(
                    tiles[piece], held.at[j, pl.ds(start, size)], sems.at[n]
                )
            )
            n += 1
        copies.append(group)
    return copies


def aggregate_kernel(lists, slots, place, target, live, used, panels, over, *refs):
    pieces = sum(len(x) for x in lists[1])
    tiles = refs[:pieces]
    out, held, panel, acc, sems, row_sems = refs[pieces:]
    blocks = out.shape[0]
    rows, main = panels.shape[:2]
    extra = over.shape[1]
    half = main // 2
    first = pltpu.make_async_copy(
        panels.at[:, pl.ds(0, half)], panel.at[pl.ds(0, rows), pl.ds(0, half)], sems.at[pieces]
    )
    first.start()

    def late(r):
        return pltpu.make_async_copy(
            panels.at[r, pl.ds(half, main - half)],
            panel.at[r, pl.ds(half, main - half)],
            row_sems.at[r, 0],
        )

    def more(r):
        return pltpu.make_async_copy(over.at[r], panel.at[r, pl.ds(main, extra)], row_sems.at[r, 1])

    def start(r):
        pl.when(used[r] > half)(lambda: late(r).start())
        pl.when(used[r] > main)(lambda: more(r).start())

    def finish(r):
        pl.when(used[r] > half)(lambda: late(r).wait())
        pl.when(used[r] > main)(lambda: more(r).wait())

    each_row(rows, 0, start)
    copies = tile_copies(lists, tiles, held, sems)
    for group in copies:
        for c in group:
            c.start()
    acc[...] = jnp.zeros_like(acc)

    each_row(rows, 0, finish)
    first.wait()
    for j in range(lists[0]):
        for c in copies[j]:
            c.wait()

        def body(g, carry, j=j):
            base = g * GROUP
            products = []
            for u in range(GROUP):
                s = j * slots + base + u
                products.append(
                    lax.dot_general(
                        panel[place[s] >> 6, place[s] & 63],
                        held[j, base + u],
                        (((1,), (1,)), ((), ())),
                        preferred_element_type=F32,
                    )
                )
            for u in range(GROUP):
                t = target[j * slots + base + u]
                acc[u % 2, t] = acc[u % 2, t] + products[u]
            return carry

        lax.fori_loop(0, (live[j] + GROUP - 1) // GROUP, body, 0)
    for t in range(blocks):
        out[t] = (acc[0, t] + acc[1, t]).astype(BF)


def aggregate(panels, over, tiles, lists, slots, place, target, live, used, blocks):
    size = tiles[0].shape[1]
    rows, main, width, _ = panels.shape
    extra = over.shape[1]
    any_spec = pl.BlockSpec(memory_space=pl.ANY)
    return pl.pallas_call(
        functools.partial(aggregate_kernel, lists, slots),
        grid_spec=pltpu.PrefetchScalarGridSpec(
            num_scalar_prefetch=4,
            grid=(1,),
            in_specs=[any_spec] * (len(tiles) + 2),
            out_specs=pl.BlockSpec((blocks, width, size), lambda i, *_: (0, 0, 0)),
            scratch_shapes=[
                pltpu.VMEM((lists[0], slots, size, size), BF),
                pltpu.VMEM((rows + 1, main + extra, width, size), BF),
                pltpu.VMEM((2, blocks + 1, width, size), F32),
                pltpu.SemaphoreType.DMA((len(tiles) + 1,)),
                pltpu.SemaphoreType.DMA((rows, 2)),
            ],
        ),
        out_shape=jax.ShapeDtypeStruct((blocks, width, size), BF),
        compiler_params=params(),
        cost_estimate=pl.CostEstimate(
            flops=2 * lists[0] * slots * width * size * size,
            bytes_accessed=rows * main * width * size * 2 + lists[0] * slots * size * size * 2,
            transcendentals=0,
        ),
    )(place, target, live, used, panels, over, *tiles)


def middle_kernel(step, weight, a0, a1, a2, a3, c0, c1, c2, c3, act, grad, wgrad, wsum):
    width = a0.shape[1]
    x = jnp.concatenate(
        [jnp.concatenate([a[b] for b in range(step)], axis=1) for a in (a0, a1, a2, a3)], axis=0
    )
    w = weight[...]
    preact = jnp.dot(w, x, preferred_element_type=F32)
    positive = jnp.maximum(preact, 0.0)
    own = positive[:width]
    act[...] = (own * own).astype(BF)
    cot = jnp.concatenate([c[...] for c in (c0, c1, c2, c3)], axis=0)
    pre = (2.0 * cot.astype(F32) * positive).astype(BF)
    g = lax.dot_general(
        w[:, :width], pre, (((0,), (0,)), ((), ())), preferred_element_type=F32
    ).astype(BF)
    for b in range(step):
        grad[b] = g[:, b * 128 : (b + 1) * 128]
    part = lax.dot_general(
        pre[:width], x, (((1,), (1,)), ((), ())), preferred_element_type=F32
    )

    @pl.when(pl.program_id(0) == 0)
    def _():
        wsum[...] = part

    @pl.when(pl.program_id(0) > 0)
    def _():
        wsum[...] = wsum[...] + part

    @pl.when(pl.program_id(0) == pl.num_programs(0) - 1)
    def _():
        for h in range(part.shape[1] // 128):
            wgrad[h * width : (h + 1) * width, :] = wsum[:, h * 128 : (h + 1) * 128].astype(BF)


def middle(weight, aggregated, cotangent):
    blocks, width, size = aggregated[0].shape
    hidden = weight.shape[0]
    step = 8 if blocks % 8 == 0 else 1
    a_spec = pl.BlockSpec((step, width, size), lambda i: (i, 0, 0))
    c_spec = pl.BlockSpec((width, step * size), lambda i: (0, i))
    tall = width * hidden // 128
    w_spec = pl.BlockSpec((tall, 128), lambda i: (0, 0))
    return pl.pallas_call(
        functools.partial(middle_kernel, step),
        grid=(blocks // step,),
        in_specs=[pl.BlockSpec((hidden, hidden), lambda i: (0, 0))] + [a_spec] * 4 + [c_spec] * 4,
        out_specs=[c_spec, a_spec, w_spec],
        out_shape=[
            jax.ShapeDtypeStruct((width, blocks * size), BF),
            jax.ShapeDtypeStruct((blocks, width, size), BF),
            jax.ShapeDtypeStruct((tall, 128), BF),
        ],
        scratch_shapes=[pltpu.VMEM((width, hidden), F32)],
        compiler_params=pltpu.CompilerParams(vmem_limit_bytes=28 * 1024 * 1024),
        cost_estimate=pl.CostEstimate(
            flops=2 * hidden * (hidden + 2 * width) * blocks * size,
            bytes_accessed=10 * blocks * width * size * 2,
            transcendentals=0,
        ),
    )(weight, *aggregated, *cotangent)


def terms_kernel(lists, slots, half, place, target, again, live, used, grads, shares, *refs):
    pieces = sum(len(x) for x in lists[1])
    tiles = refs[:pieces]
    out, over, held, made, sems, row_sems = refs[pieces:]
    rows, tall = out.shape[:2]
    extra = over.shape[1]
    width = grads.shape[1]
    copies = tile_copies(lists, tiles, held, sems)
    for group in copies:
        for c in group:
            c.start()
    for r in range(rows):
        h = r % (shares.shape[0] // EDGE)
        made[r, :EDGE, :] = shares[h * EDGE : (h + 1) * EDGE, :]
    for j in range(lists[0]):
        for c in copies[j]:
            c.wait()

        def body(g, carry, j=j):
            base = g * GROUP
            products = []
            for u in range(GROUP):
                s = j * slots + base + u
                t = jnp.minimum(target[s], grads.shape[0] - 1)
                products.append(
                    jnp.dot(grads[t], held[j, base + u], preferred_element_type=F32)
                )
            plain = again[j * slots + base]
            for u in range(1, GROUP):
                plain = plain + again[j * slots + base + u]

            def put(u, keep):
                s = j * slots + base + u
                at = pl.ds(pl.multiple_of(EDGE + (place[s] & 63) * width, EDGE), width)
                p = place[s] >> 6
                value = products[u]
                if keep:
                    value = value + jnp.where(again[s] > 0, made[p, at, :].astype(F32), 0.0)
                made[p, at, :] = value.astype(BF)

            @pl.when(plain == 0)
            def _():
                for u in range(GROUP):
                    put(u, False)

            @pl.when(plain > 0)
            def _():
                for u in range(GROUP):
                    put(u, True)

            return carry

        lax.fori_loop(0, (live[j] + GROUP - 1) // GROUP, body, 0)
    first = EDGE + half * width
    whole = pltpu.make_async_copy(
        made.at[pl.ds(0, rows), pl.ds(0, first)], out.at[:, pl.ds(0, first)], sems.at[pieces]
    )
    whole.start()

    def late(r):
        span = pl.ds(first, tall - first)
        return pltpu.make_async_copy(made.at[r, span], out.at[r, span], row_sems.at[r, 0])

    def more(r):
        return pltpu.make_async_copy(made.at[r, pl.ds(tall, extra)], over.at[r], row_sems.at[r, 1])

    def start(r):
        pl.when(used[r] > half)(lambda: late(r).start())
        pl.when(used[r] > 2 * half)(lambda: more(r).start())

    def finish(r):
        pl.when(used[r] > half)(lambda: late(r).wait())
        pl.when(used[r] > 2 * half)(lambda: more(r).wait())

    each_row(rows, 0, start)
    each_row(rows, 0, finish)
    whole.wait()


def terms(grads, shares, tiles, lists, slots, place, target, again, live, used, rows, main, extra):
    size = tiles[0].shape[1]
    blocks, width, _ = grads.shape
    any_spec = pl.BlockSpec(memory_space=pl.ANY)
    return pl.pallas_call(
        functools.partial(terms_kernel, lists, slots, main // 2),
        grid_spec=pltpu.PrefetchScalarGridSpec(
            num_scalar_prefetch=5,
            grid=(1,),
            in_specs=[
                pl.BlockSpec((blocks, width, size), lambda i, *_: (0, 0, 0)),
                pl.BlockSpec(shares.shape, lambda i, *_: (0, 0)),
            ]
            + [any_spec] * len(tiles),
            out_specs=[any_spec, any_spec],
            scratch_shapes=[
                pltpu.VMEM((lists[0], slots, size, size), BF),
                pltpu.VMEM((rows + 1, EDGE + (main + extra) * width, size), BF),
                pltpu.SemaphoreType.DMA((len(tiles) + 1,)),
                pltpu.SemaphoreType.DMA((rows, 2)),
            ],
        ),
        out_shape=[
            jax.ShapeDtypeStruct((rows, EDGE + main * width, size), BF),
            jax.ShapeDtypeStruct((rows, extra * width, size), BF),
        ],
        compiler_params=params(),
        cost_estimate=pl.CostEstimate(
            flops=2 * lists[0] * slots * width * size * size,
            bytes_accessed=rows * main * width * size * 2 + lists[0] * slots * size * size * 2,
            transcendentals=0,
        ),
    )(place, target, again, live, used, grads, shares, *tiles)


def collect_kernel(chains, spans, blocks, index, count, incoming, over, out, buf, acc, sems):
    width = out.shape[0]
    rows = incoming.shape[0]
    main = spans[-1][0]

    def came(r, n):
        low, high = spans[n]
        if low >= main:
            source = over.at[r]
        else:
            source = incoming.at[r, pl.ds(EDGE + low * width, (high - low) * width)]
        return pltpu.make_async_copy(
            source, buf.at[r, pl.ds(low * width, (high - low) * width)], sems.at[r, n]
        )

    def spread(act, r):
        act(r, 0)
        for n in (1, 2):
            pl.when(count[r] > spans[n][0])(functools.partial(act, r, n))

    each_row(rows, 0, functools.partial(spread, lambda r, n: came(r, n).start()))
    acc[...] = jnp.zeros_like(acc)

    def add(g, n):
        for k in range(*spans[n]):
            for q in range(chains):
                r = g * chains + q
                t = index[r, k]
                acc[q, t] = acc[q, t] + buf[r, k * width : (k + 1) * width, :].astype(F32)

    def body(g):
        most = count[g * chains]
        for q in range(chains):
            spread(lambda r, n: came(r, n).wait(), g * chains + q)
            most = jnp.maximum(most, count[g * chains + q])
        add(g, 0)
        for n in (1, 2):
            pl.when(most > spans[n][0])(functools.partial(add, g, n))

    each_row(rows // chains, 0, body)
    for b in range(blocks):
        total = acc[0, b]
        for q in range(1, chains):
            total = total + acc[q, b]
        out[:, b * 128 : (b + 1) * 128] = total.astype(BF)


def collect(incoming, over, index, count, blocks, width, main, extra):
    rows = incoming.shape[0]
    chains = 4
    any_spec = pl.BlockSpec(memory_space=pl.ANY)
    spans = ((0, main // 2), (main // 2, main), (main, main + extra))
    return pl.pallas_call(
        functools.partial(collect_kernel, chains, spans, blocks),
        grid_spec=pltpu.PrefetchScalarGridSpec(
            num_scalar_prefetch=2,
            grid=(1,),
            in_specs=[any_spec, any_spec],
            out_specs=pl.BlockSpec((width, blocks * 128), lambda r, *_: (0, 0)),
            scratch_shapes=[
                pltpu.VMEM((rows, (main + extra) * width, 128), BF),
                pltpu.VMEM((chains, blocks + 1, width, 128), F32),
                pltpu.SemaphoreType.DMA((rows, 3)),
            ],
        ),
        out_shape=jax.ShapeDtypeStruct((width, blocks * 128), BF),
        compiler_params=params(),
        cost_estimate=pl.CostEstimate(
            flops=rows * main * width * 128,
            bytes_accessed=rows * main * width * 256,
            transcendentals=0,
        ),
    )(index, count, incoming, over)


def exchange(x):
    return lax.all_to_all(x, "rows", split_axis=0, concat_axis=0, tiled=True)


def exchange_both(main, over, needed):
    over = lax.cond(needed, exchange, lambda x: x, over)
    main, over = lax.optimization_barrier((main, over))
    return exchange(main), over


def share_total_kernel(incoming, out):
    total = incoming[0].astype(F32)
    for r in range(1, incoming.shape[0]):
        total = total + incoming[r].astype(F32)
    out[...] = total


def share_total(returned):
    rows = returned.shape[0]
    return pl.pallas_call(
        share_total_kernel,
        grid=(1,),
        in_specs=[pl.BlockSpec((rows, EDGE, 128), lambda i: (0, 0, 0))],
        out_specs=pl.BlockSpec((EDGE, 128), lambda i: (0, 0)),
        out_shape=jax.ShapeDtypeStruct((EDGE, 128), F32),
        compiler_params=params(),
    )(returned)


def share_sum(piece, parts, rows):
    row = lax.axis_index("rows")
    have = [piece] + [
        lax.ppermute(piece, "rows", [(i, i ^ k) for i in range(rows)]) for k in range(1, parts)
    ]
    bit = 1
    while bit < parts:
        odd = (row & bit) > 0
        have = [jnp.where(odd, have[i ^ bit], have[i]) for i in range(parts)]
        bit *= 2
    return have


def on_device(features, weight, cotangent, blocks, row_block, src_owner, src_block, live):
    rows = lax.axis_size("rows")
    feats = lax.axis_size("feat")
    me = lax.axis_index("feat")
    width, nodes = features.shape
    size = blocks.shape[2]
    slots = blocks.shape[1]
    local = nodes // size
    most = max(2, 2 * slots // rows) * feats
    extra = EXTRA
    main = most - extra
    head = HEAD

    own_tiles = blocks[0]
    far_head = chip_swap(own_tiles[:head])

    here = jnp.arange(slots, dtype=I32)
    alive = here < live[0, 0]
    code = jnp.where(alive, src_owner[0, :, 0] * 64 + src_block[0], -1)
    goal = jnp.where(alive, row_block[0], local)
    note = gather_feat(jnp.stack([code, goal]))
    code = jnp.concatenate([n[0] for n in note])
    target = jnp.concatenate([n[1] for n in note])
    valid = code >= 0
    owner = jnp.where(valid, code >> 6, -1)
    block = jnp.where(valid, code & 63, -1)
    owner_hot = owner[:, None] == jnp.arange(rows, dtype=I32)[None, :]
    block_hot = block[:, None] == jnp.arange(local, dtype=I32)[None, :]
    want = exact_dot(owner_hot.T, block_hot) > 0.5
    rank = ranks(want)
    used = jnp.sum(want.astype(I32), axis=1)
    largest = jnp.max(used)
    request = jnp.concatenate(
        [want.astype(I32), jnp.broadcast_to(largest, (rows, 128 - local))], axis=1
    )
    weights = relative(jnp.concatenate(gather_feat(weight), axis=0), 1, me)

    slot_rank = jnp.sum(jnp.where(block_hot, exact_dot(owner_hot, rank), 0.0), axis=1).astype(I32)
    place = jnp.where(valid, owner * 64 + slot_rank, rows * 64)
    order = jnp.arange(feats * slots, dtype=I32)
    again = jnp.any(
        (code[:, None] == code[None, :]) & (order[None, :] < order[:, None]), axis=1
    ).astype(I32)
    counts = jnp.sum(valid.astype(I32).reshape(feats, slots), axis=1)
    answer = exchange(request)
    answer, far_head, weights, place, again, counts, target = lax.optimization_barrier(
        (answer, far_head, weights, place, again, counts, target)
    )
    asked = answer[:, :local]
    needed = jnp.max(answer[:, local]) > main
    asked_rank = ranks(asked)
    asked_count = jnp.sum(asked, axis=1)
    at = jnp.arange(STRIDE, dtype=I32)[None, :, None]
    chosen = (asked[:, None, :] > 0) & (asked_rank[:, None, :] == at)
    index = local + jnp.sum(jnp.where(chosen, jnp.arange(local, dtype=I32) - local, 0), axis=2)
    served, over = serve(features, index, asked_count, rows, main, extra)
    panels, over = exchange_both(served, over, needed)
    panels = panels.reshape(rows, main, width, size)
    over = over.reshape(rows, extra, width, size)

    far_tail, cotangent, answer = lax.optimization_barrier((own_tiles[head:], cotangent, answer))
    far_tail = chip_swap(far_tail)
    tiles = (
        own_tiles,
        core_swap(own_tiles),
        far_head,
        far_tail,
        core_swap(far_head),
        core_swap(far_tail),
    )
    lists = (
        feats,
        (
            ((0, 0, slots),),
            ((1, 0, slots),),
            ((2, 0, head), (3, head, slots - head)),
            ((4, 0, head), (5, head, slots - head)),
        ),
    )
    cotangents = gather_feat(cotangent)

    own = aggregate(panels, over, tiles, lists, slots, place, target, counts, used, local)
    aggregated = gather_feat(own)
    activation, grads, shares = middle(weights, aggregated, cotangents)
    made, over = terms(
        grads, shares, tiles, lists, slots, place, target, again, counts, used, rows, main, extra
    )
    returned, over = exchange_both(made, over, needed)
    piece = share_total(returned)
    total = jnp.concatenate(share_sum(piece, shares.shape[0] // EDGE, rows), axis=0)
    total = jnp.concatenate(jnp.split(total, total.shape[0] // width, axis=0), axis=1)
    weight_grad = relative(total, 1, me) * (1.0 / math.sqrt(nodes * rows))
    feature_grad = collect(returned, over, index, asked_count, local, width, main, extra)
    return (activation, feature_grad, weight_grad)


def solution(mesh):
    placed = (
        P("feat", "rows"),
        P("feat", None),
        P("feat", "rows"),
        P("rows", "feat", None, None),
        P("rows", "feat"),
        P("rows", "feat", None),
        P("rows", "feat"),
        P("rows", "feat"),
    )
    return jax.shard_map(
        on_device,
        mesh=mesh,
        in_specs=placed,
        out_specs=(P("feat", "rows"), P("feat", "rows"), P("feat", None)),
        check_vma=False,
    )
```

```python
import functools
import math

import jax
import jax.numpy as jnp
from jax import lax
from jax.experimental import pallas as pl
from jax.experimental.pallas import tpu as pltpu
from jax.sharding import PartitionSpec as P

BF = jnp.bfloat16
F32 = jnp.float32
I32 = jnp.int32
VMEM_LIMIT = 56 * 1024 * 1024
GROUP = 8
STRIDE = 16
EDGE = 32
EXTRA = 2
HEAD = 32


def params():
    return pltpu.CompilerParams(vmem_limit_bytes=VMEM_LIMIT)


def core_swap(x):
    return lax.ppermute(x, "feat", [(0, 1), (1, 0), (2, 3), (3, 2)])


def chip_swap(x):
    return lax.ppermute(x, "feat", [(0, 2), (2, 0), (1, 3), (3, 1)])


def gather_feat(x):
    far = chip_swap(x)
    return (x, core_swap(x), far, core_swap(far))


def relative(x, axis, me):
    a = jnp.split(x, 4, axis=axis)
    low = (me & 1) == 1
    high = (me & 2) == 2
    b = [jnp.where(low, a[i ^ 1], a[i]) for i in range(4)]
    c = [jnp.where(high, b[i ^ 2], b[i]) for i in range(4)]
    return jnp.concatenate(c, axis=axis)


def exact_dot(a, b):
    return jnp.dot(a.astype(BF), b.astype(BF), preferred_element_type=F32)


def ranks(want):
    n = want.shape[-1]
    upper = jnp.arange(n)[:, None] < jnp.arange(n)[None, :]
    return exact_dot(want, upper).astype(I32)


def each_row(rows, first, act):
    def body(r, carry):
        act(r)
        return carry

    lax.fori_loop(first, rows, body, 0)


def serve_kernel(spans, index, count, features, out, over, buf, sems):
    width = features.shape[0]
    rows = out.shape[0]
    main = spans[-1][0]

    def sent(r, n):
        low, high = spans[n]
        ref, base = (over, main) if low >= main else (out, 0)
        return pltpu.make_async_copy(
            buf.at[r, pl.ds(low * width, (high - low) * width)],
            ref.at[r, pl.ds((low - base) * width, (high - low) * width)],
            sems.at[r, n],
        )

    def fill(r, n):
        for k in range(*spans[n]):
            block = jnp.minimum(index[r, k], features.shape[1] // 128 - 1)
            start = pl.multiple_of(block * 128, 128)
            buf[r, k * width : (k + 1) * width, :] = features[:, pl.ds(start, 128)]
        sent(r, n).start()

    def spread(act):
        def body(r):
            act(r, 0)
            for n in (1, 2):
                pl.when(count[r] > spans[n][0])(functools.partial(act, r, n))

        each_row(rows, 0, body)

    spread(fill)
    spread(lambda r, n: sent(r, n).wait())


def serve(features, index, count, rows, main, extra):
    width, nodes = features.shape
    any_spec = pl.BlockSpec(memory_space=pl.ANY)
    spans = ((0, main // 2), (main // 2, main), (main, main + extra))
    return pl.pallas_call(
        functools.partial(serve_kernel, spans),
        grid_spec=pltpu.PrefetchScalarGridSpec(
            num_scalar_prefetch=2,
            grid=(1,),
            in_specs=[pl.BlockSpec((width, nodes), lambda r, *_: (0, 0))],
            out_specs=[any_spec, any_spec],
            scratch_shapes=[
                pltpu.VMEM((rows, (main + extra) * width, 128), BF),
                pltpu.SemaphoreType.DMA((rows, 3)),
            ],
        ),
        out_shape=[
            jax.ShapeDtypeStruct((rows, main * width, 128), BF),
            jax.ShapeDtypeStruct((rows, extra * width, 128), BF),
        ],
        compiler_params=params(),
        cost_estimate=pl.CostEstimate(
            flops=0, bytes_accessed=rows * (main + extra) * width * 256, transcendentals=0
        ),
    )(index, count, features)


def tile_copies(lists, tiles, held, sems):
    copies, n = [], 0
    for j in range(lists[0]):
        group = []
        for piece, start, size in lists[1][j]:
            group.append(
                pltpu.make_async_copy(
                    tiles[piece], held.at[j, pl.ds(start, size)], sems.at[n]
                )
            )
            n += 1
        copies.append(group)
    return copies


def aggregate_kernel(lists, slots, place, target, live, used, panels, over, *refs):
    pieces = sum(len(x) for x in lists[1])
    tiles = refs[:pieces]
    out, held, panel, acc, sems, row_sems = refs[pieces:]
    blocks = out.shape[0]
    rows, main = panels.shape[:2]
    extra = over.shape[1]
    half = main // 2
    first = pltpu.make_async_copy(
        panels.at[:, pl.ds(0, half)], panel.at[pl.ds(0, rows), pl.ds(0, half)], sems.at[pieces]
    )
    first.start()

    def late(r):
        return pltpu.make_async_copy(
            panels.at[r, pl.ds(half, main - half)],
            panel.at[r, pl.ds(half, main - half)],
            row_sems.at[r, 0],
        )

    def more(r):
        return pltpu.make_async_copy(over.at[r], panel.at[r, pl.ds(main, extra)], row_sems.at[r, 1])

    def start(r):
        pl.when(used[r] > half)(lambda: late(r).start())
        pl.when(used[r] > main)(lambda: more(r).start())

    def finish(r):
        pl.when(used[r] > half)(lambda: late(r).wait())
        pl.when(used[r] > main)(lambda: more(r).wait())

    each_row(rows, 0, start)
    copies = tile_copies(lists, tiles, held, sems)
    for group in copies:
        for c in group:
            c.start()
    acc[...] = jnp.zeros_like(acc)

    each_row(rows, 0, finish)
    first.wait()
    for j in range(lists[0]):
        for c in copies[j]:
            c.wait()

        def body(g, carry, j=j):
            base = g * GROUP
            products = []
            for u in range(GROUP):
                s = j * slots + base + u
                products.append(
                    lax.dot_general(
                        panel[place[s] >> 6, place[s] & 63],
                        held[j, base + u],
                        (((1,), (1,)), ((), ())),
                        preferred_element_type=F32,
                    )
                )
            for u in range(GROUP):
                t = target[j * slots + base + u]
                acc[u % 2, t] = acc[u % 2, t] + products[u]
            return carry

        lax.fori_loop(0, (live[j] + GROUP - 1) // GROUP, body, 0)
    for t in range(blocks):
        out[t] = (acc[0, t] + acc[1, t]).astype(BF)


def aggregate(panels, over, tiles, lists, slots, place, target, live, used, blocks):
    size = tiles[0].shape[1]
    rows, main, width, _ = panels.shape
    extra = over.shape[1]
    any_spec = pl.BlockSpec(memory_space=pl.ANY)
    return pl.pallas_call(
        functools.partial(aggregate_kernel, lists, slots),
        grid_spec=pltpu.PrefetchScalarGridSpec(
            num_scalar_prefetch=4,
            grid=(1,),
            in_specs=[any_spec] * (len(tiles) + 2),
            out_specs=pl.BlockSpec((blocks, width, size), lambda i, *_: (0, 0, 0)),
            scratch_shapes=[
                pltpu.VMEM((lists[0], slots, size, size), BF),
                pltpu.VMEM((rows + 1, main + extra, width, size), BF),
                pltpu.VMEM((2, blocks + 1, width, size), F32),
                pltpu.SemaphoreType.DMA((len(tiles) + 1,)),
                pltpu.SemaphoreType.DMA((rows, 2)),
            ],
        ),
        out_shape=jax.ShapeDtypeStruct((blocks, width, size), BF),
        compiler_params=params(),
        cost_estimate=pl.CostEstimate(
            flops=2 * lists[0] * slots * width * size * size,
            bytes_accessed=rows * main * width * size * 2 + lists[0] * slots * size * size * 2,
            transcendentals=0,
        ),
    )(place, target, live, used, panels, over, *tiles)


def middle_kernel(step, weight, a0, a1, a2, a3, c0, c1, c2, c3, act, grad, wgrad, wsum):
    width = a0.shape[1]
    x = jnp.concatenate(
        [jnp.concatenate([a[b] for b in range(step)], axis=1) for a in (a0, a1, a2, a3)], axis=0
    )
    w = weight[...]
    preact = jnp.dot(w, x, preferred_element_type=F32)
    positive = jnp.maximum(preact, 0.0)
    own = positive[:width]
    act[...] = (own * own).astype(BF)
    cot = jnp.concatenate([c[...] for c in (c0, c1, c2, c3)], axis=0)
    pre = (2.0 * cot.astype(F32) * positive).astype(BF)
    g = lax.dot_general(
        w[:, :width], pre, (((0,), (0,)), ((), ())), preferred_element_type=F32
    ).astype(BF)
    for b in range(step):
        grad[b] = g[:, b * 128 : (b + 1) * 128]
    part = lax.dot_general(
        pre[:width], x, (((1,), (1,)), ((), ())), preferred_element_type=F32
    )

    @pl.when(pl.program_id(0) == 0)
    def _():
        wsum[...] = part

    @pl.when(pl.program_id(0) > 0)
    def _():
        wsum[...] = wsum[...] + part

    @pl.when(pl.program_id(0) == pl.num_programs(0) - 1)
    def _():
        for h in range(part.shape[1] // 128):
            wgrad[h * width : (h + 1) * width, :] = wsum[:, h * 128 : (h + 1) * 128].astype(BF)


def middle(weight, aggregated, cotangent):
    blocks, width, size = aggregated[0].shape
    hidden = weight.shape[0]
    step = 8 if blocks % 8 == 0 else 1
    a_spec = pl.BlockSpec((step, width, size), lambda i: (i, 0, 0))
    c_spec = pl.BlockSpec((width, step * size), lambda i: (0, i))
    tall = width * hidden // 128
    w_spec = pl.BlockSpec((tall, 128), lambda i: (0, 0))
    return pl.pallas_call(
        functools.partial(middle_kernel, step),
        grid=(blocks // step,),
        in_specs=[pl.BlockSpec((hidden, hidden), lambda i: (0, 0))] + [a_spec] * 4 + [c_spec] * 4,
        out_specs=[c_spec, a_spec, w_spec],
        out_shape=[
            jax.ShapeDtypeStruct((width, blocks * size), BF),
            jax.ShapeDtypeStruct((blocks, width, size), BF),
            jax.ShapeDtypeStruct((tall, 128), BF),
        ],
        scratch_shapes=[pltpu.VMEM((width, hidden), F32)],
        compiler_params=pltpu.CompilerParams(vmem_limit_bytes=28 * 1024 * 1024),
        cost_estimate=pl.CostEstimate(
            flops=2 * hidden * (hidden + 2 * width) * blocks * size,
            bytes_accessed=10 * blocks * width * size * 2,
            transcendentals=0,
        ),
    )(weight, *aggregated, *cotangent)


def terms_kernel(lists, slots, half, place, target, again, live, used, grads, shares, *refs):
    pieces = sum(len(x) for x in lists[1])
    tiles = refs[:pieces]
    out, over, held, made, sems, row_sems = refs[pieces:]
    rows, tall = out.shape[:2]
    extra = over.shape[1]
    width = grads.shape[1]
    copies = tile_copies(lists, tiles, held, sems)
    for group in copies:
        for c in group:
            c.start()
    for r in range(rows):
        h = r % (shares.shape[0] // EDGE)
        made[r, :EDGE, :] = shares[h * EDGE : (h + 1) * EDGE, :]
    for j in range(lists[0]):
        for c in copies[j]:
            c.wait()

        def body(g, carry, j=j):
            base = g * GROUP
            products = []
            for u in range(GROUP):
                s = j * slots + base + u
                t = jnp.minimum(target[s], grads.shape[0] - 1)
                products.append(
                    jnp.dot(grads[t], held[j, base + u], preferred_element_type=F32)
                )
            plain = again[j * slots + base]
            for u in range(1, GROUP):
                plain = plain + again[j * slots + base + u]

            def put(u, keep):
                s = j * slots + base + u
                at = pl.ds(pl.multiple_of(EDGE + (place[s] & 63) * width, EDGE), width)
                p = place[s] >> 6
                value = products[u]
                if keep:
                    value = value + jnp.where(again[s] > 0, made[p, at, :].astype(F32), 0.0)
                made[p, at, :] = value.astype(BF)

            @pl.when(plain == 0)
            def _():
                for u in range(GROUP):
                    put(u, False)

            @pl.when(plain > 0)
            def _():
                for u in range(GROUP):
                    put(u, True)

            return carry

        lax.fori_loop(0, (live[j] + GROUP - 1) // GROUP, body, 0)
    first = EDGE + half * width
    whole = pltpu.make_async_copy(
        made.at[pl.ds(0, rows), pl.ds(0, first)], out.at[:, pl.ds(0, first)], sems.at[pieces]
    )
    whole.start()

    def late(r):
        span = pl.ds(first, tall - first)
        return pltpu.make_async_copy(made.at[r, span], out.at[r, span], row_sems.at[r, 0])

    def more(r):
        return pltpu.make_async_copy(made.at[r, pl.ds(tall, extra)], over.at[r], row_sems.at[r, 1])

    def start(r):
        pl.when(used[r] > half)(lambda: late(r).start())
        pl.when(used[r] > 2 * half)(lambda: more(r).start())

    def finish(r):
        pl.when(used[r] > half)(lambda: late(r).wait())
        pl.when(used[r] > 2 * half)(lambda: more(r).wait())

    each_row(rows, 0, start)
    each_row(rows, 0, finish)
    whole.wait()


def terms(grads, shares, tiles, lists, slots, place, target, again, live, used, rows, main, extra):
    size = tiles[0].shape[1]
    blocks, width, _ = grads.shape
    any_spec = pl.BlockSpec(memory_space=pl.ANY)
    return pl.pallas_call(
        functools.partial(terms_kernel, lists, slots, main // 2),
        grid_spec=pltpu.PrefetchScalarGridSpec(
            num_scalar_prefetch=5,
            grid=(1,),
            in_specs=[
                pl.BlockSpec((blocks, width, size), lambda i, *_: (0, 0, 0)),
                pl.BlockSpec(shares.shape, lambda i, *_: (0, 0)),
            ]
            + [any_spec] * len(tiles),
            out_specs=[any_spec, any_spec],
            scratch_shapes=[
                pltpu.VMEM((lists[0], slots, size, size), BF),
                pltpu.VMEM((rows + 1, EDGE + (main + extra) * width, size), BF),
                pltpu.SemaphoreType.DMA((len(tiles) + 1,)),
                pltpu.SemaphoreType.DMA((rows, 2)),
            ],
        ),
        out_shape=[
            jax.ShapeDtypeStruct((rows, EDGE + main * width, size), BF),
            jax.ShapeDtypeStruct((rows, extra * width, size), BF),
        ],
        compiler_params=params(),
        cost_estimate=pl.CostEstimate(
            flops=2 * lists[0] * slots * width * size * size,
            bytes_accessed=rows * main * width * size * 2 + lists[0] * slots * size * size * 2,
            transcendentals=0,
        ),
    )(place, target, again, live, used, grads, shares, *tiles)


def collect_kernel(chains, spans, blocks, index, count, incoming, over, out, buf, acc, sems):
    width = out.shape[0]
    rows = incoming.shape[0]
    main = spans[-1][0]

    def came(r, n):
        low, high = spans[n]
        if low >= main:
            source = over.at[r]
        else:
            source = incoming.at[r, pl.ds(EDGE + low * width, (high - low) * width)]
        return pltpu.make_async_copy(
            source, buf.at[r, pl.ds(low * width, (high - low) * width)], sems.at[r, n]
        )

    def spread(act, r):
        act(r, 0)
        for n in (1, 2):
            pl.when(count[r] > spans[n][0])(functools.partial(act, r, n))

    each_row(rows, 0, functools.partial(spread, lambda r, n: came(r, n).start()))
    acc[...] = jnp.zeros_like(acc)

    def add(g, n):
        for k in range(*spans[n]):
            for q in range(chains):
                r = g * chains + q
                t = index[r, k]
                acc[q, t] = acc[q, t] + buf[r, k * width : (k + 1) * width, :].astype(F32)

    def body(g):
        most = count[g * chains]
        for q in range(chains):
            spread(lambda r, n: came(r, n).wait(), g * chains + q)
            most = jnp.maximum(most, count[g * chains + q])
        add(g, 0)
        for n in (1, 2):
            pl.when(most > spans[n][0])(functools.partial(add, g, n))

    each_row(rows // chains, 0, body)
    for b in range(blocks):
        total = acc[0, b]
        for q in range(1, chains):
            total = total + acc[q, b]
        out[:, b * 128 : (b + 1) * 128] = total.astype(BF)


def collect(incoming, over, index, count, blocks, width, main, extra):
    rows = incoming.shape[0]
    chains = 4
    any_spec = pl.BlockSpec(memory_space=pl.ANY)
    spans = ((0, main // 2), (main // 2, main), (main, main + extra))
    return pl.pallas_call(
        functools.partial(collect_kernel, chains, spans, blocks),
        grid_spec=pltpu.PrefetchScalarGridSpec(
            num_scalar_prefetch=2,
            grid=(1,),
            in_specs=[any_spec, any_spec],
            out_specs=pl.BlockSpec((width, blocks * 128), lambda r, *_: (0, 0)),
            scratch_shapes=[
                pltpu.VMEM((rows, (main + extra) * width, 128), BF),
                pltpu.VMEM((chains, blocks + 1, width, 128), F32),
                pltpu.SemaphoreType.DMA((rows, 3)),
            ],
        ),
        out_shape=jax.ShapeDtypeStruct((width, blocks * 128), BF),
        compiler_params=params(),
        cost_estimate=pl.CostEstimate(
            flops=rows * main * width * 128,
            bytes_accessed=rows * main * width * 256,
            transcendentals=0,
        ),
    )(index, count, incoming, over)


def exchange(x):
    return lax.all_to_all(x, "rows", split_axis=0, concat_axis=0, tiled=True)


def exchange_both(main, over, needed):
    over = lax.cond(needed, exchange, lambda x: x, over)
    main, over = lax.optimization_barrier((main, over))
    return exchange(main), over


def share_total_kernel(incoming, out):
    total = incoming[0].astype(F32)
    for r in range(1, incoming.shape[0]):
        total = total + incoming[r].astype(F32)
    out[...] = total


def share_total(returned):
    rows = returned.shape[0]
    return pl.pallas_call(
        share_total_kernel,
        grid=(1,),
        in_specs=[pl.BlockSpec((rows, EDGE, 128), lambda i: (0, 0, 0))],
        out_specs=pl.BlockSpec((EDGE, 128), lambda i: (0, 0)),
        out_shape=jax.ShapeDtypeStruct((EDGE, 128), F32),
        compiler_params=params(),
    )(returned)


def share_sum(piece, parts, rows):
    row = lax.axis_index("rows")
    have = [piece] + [
        lax.ppermute(piece, "rows", [(i, i ^ k) for i in range(rows)]) for k in range(1, parts)
    ]
    bit = 1
    while bit < parts:
        odd = (row & bit) > 0
        have = [jnp.where(odd, have[i ^ bit], have[i]) for i in range(parts)]
        bit *= 2
    return have


def on_device(features, weight, cotangent, blocks, row_block, src_owner, src_block, live):
    rows = lax.axis_size("rows")
    feats = lax.axis_size("feat")
    me = lax.axis_index("feat")
    width, nodes = features.shape
    size = blocks.shape[2]
    slots = blocks.shape[1]
    local = nodes // size
    most = max(2, 2 * slots // rows) * feats
    extra = EXTRA
    main = most - extra
    head = HEAD

    own_tiles = blocks[0]
    far_head = chip_swap(own_tiles[:head])

    here = jnp.arange(slots, dtype=I32)
    alive = here < live[0, 0]
    code = jnp.where(alive, src_owner[0, :, 0] * 64 + src_block[0], -1)
    goal = jnp.where(alive, row_block[0], local)
    note = gather_feat(jnp.stack([code, goal]))
    code = jnp.concatenate([n[0] for n in note])
    target = jnp.concatenate([n[1] for n in note])
    valid = code >= 0
    owner = jnp.where(valid, code >> 6, -1)
    block = jnp.where(valid, code & 63, -1)
    owner_hot = owner[:, None] == jnp.arange(rows, dtype=I32)[None, :]
    block_hot = block[:, None] == jnp.arange(local, dtype=I32)[None, :]
    want = exact_dot(owner_hot.T, block_hot) > 0.5
    rank = ranks(want)
    used = jnp.sum(want.astype(I32), axis=1)
    largest = jnp.max(used)
    request = jnp.concatenate(
        [want.astype(I32), jnp.broadcast_to(largest, (rows, 128 - local))], axis=1
    )
    weights = relative(jnp.concatenate(gather_feat(weight), axis=0), 1, me)

    slot_rank = jnp.sum(jnp.where(block_hot, exact_dot(owner_hot, rank), 0.0), axis=1).astype(I32)
    place = jnp.where(valid, owner * 64 + slot_rank, rows * 64)
    order = jnp.arange(feats * slots, dtype=I32)
    again = jnp.any(
        (code[:, None] == code[None, :]) & (order[None, :] < order[:, None]), axis=1
    ).astype(I32)
    counts = jnp.sum(valid.astype(I32).reshape(feats, slots), axis=1)
    answer = exchange(request)
    answer, far_head, weights, place, again, counts, target = lax.optimization_barrier(
        (answer, far_head, weights, place, again, counts, target)
    )
    asked = answer[:, :local]
    needed = jnp.max(answer[:, local]) > main
    asked_rank = ranks(asked)
    asked_count = jnp.sum(asked, axis=1)
    at = jnp.arange(STRIDE, dtype=I32)[None, :, None]
    chosen = (asked[:, None, :] > 0) & (asked_rank[:, None, :] == at)
    index = local + jnp.sum(jnp.where(chosen, jnp.arange(local, dtype=I32) - local, 0), axis=2)
    served, over = serve(features, index, asked_count, rows, main, extra)
    panels, over = exchange_both(served, over, needed)
    panels = panels.reshape(rows, main, width, size)
    over = over.reshape(rows, extra, width, size)

    far_tail, cotangent, answer = lax.optimization_barrier((own_tiles[head:], cotangent, answer))
    far_tail = chip_swap(far_tail)
    tiles = (
        own_tiles,
        core_swap(own_tiles),
        far_head,
        far_tail,
        core_swap(far_head),
        core_swap(far_tail),
    )
    lists = (
        feats,
        (
            ((0, 0, slots),),
            ((1, 0, slots),),
            ((2, 0, head), (3, head, slots - head)),
            ((4, 0, head), (5, head, slots - head)),
        ),
    )
    cotangents = gather_feat(cotangent)

    own = aggregate(panels, over, tiles, lists, slots, place, target, counts, used, local)
    aggregated = gather_feat(own)
    activation, grads, shares = middle(weights, aggregated, cotangents)
    made, over = terms(
        grads, shares, tiles, lists, slots, place, target, again, counts, used, rows, main, extra
    )
    returned, over = exchange_both(made, over, needed)
    piece = share_total(returned)
    total = jnp.concatenate(share_sum(piece, shares.shape[0] // EDGE, rows), axis=0)
    total = jnp.concatenate(jnp.split(total, total.shape[0] // width, axis=0), axis=1)
    weight_grad = relative(total, 1, me) * (1.0 / math.sqrt(nodes * rows))
    feature_grad = collect(returned, over, index, asked_count, local, width, main, extra)
    return (activation, feature_grad, weight_grad)


def solution(mesh):
    placed = (
        P("feat", "rows"),
        P("feat", None),
        P("feat", "rows"),
        P("rows", "feat", None, None),
        P("rows", "feat"),
        P("rows", "feat", None),
        P("rows", "feat"),
        P("rows", "feat"),
    )
    return jax.shard_map(
        on_device,
        mesh=mesh,
        in_specs=placed,
        out_specs=(P("feat", "rows"), P("feat", "rows"), P("feat", None)),
        check_vma=False,
    )
```
